32 devices in a mesh: shard: 8 (over y, x, core), rep: 4 (over z).
Axes of the slice: x: 2, y: 2, z: 4, core: 2. Of those that a mesh axis runs over, the one named last changes fastest.
Arguments:
- inputs: bfloat16 [32768, 768], P(('shard', 'rep')), may hold values from -6 to 6
- w_query: bfloat16 [768, 768], P('shard'), may hold values from -0.21875 to 0.21875
- w_key: bfloat16 [768, 768], P('shard'), may hold values from -0.21875 to 0.21875
- w_value: bfloat16 [768, 768], P('shard'), may hold values from -0.21875 to 0.21875
- w_output: bfloat16 [768, 768], P('shard'), may hold values from -0.875 to 0.875
- w_router: bfloat16 [768, 8], P('shard'), may hold values from -0.15625 to 0.15625
- gain_attn: bfloat16 [768], P('shard'), may hold values from 0.5 to 1.5
- gain_expert: bfloat16 [768], P('shard'), may hold values from 0.5 to 1.5
- rel_bias: bfloat16 [32, 12], P('shard'), may hold values from -4 to 4
- w_in: bfloat16 [8, 768, 3072], P('shard'), may hold values from -0.21875 to 0.21875
- w_out: bfloat16 [8, 3072, 768], P('shard'), may hold values from -0.21875 to 0.21875
- segment_ids: int32 [32, 1024], P(('shard', 'rep')), may hold values from 0 to 3, never falling along the last dimension, each value on 1 to 512 neighbouring positions
- expert_ids: int32 [32768, 2], P(('shard', 'rep')), may hold values from 0 to 7, all different within a row; in each aligned block of 1024 rows (0 to 1023, 1024 to 2047, ...) at most 384 rows name the same one
- out_grad: bfloat16 [32768, 768], P(('shard', 'rep')), may hold values from -6 to 6
Outputs:
- output: bfloat16 [32768, 768], P(('shard', 'rep'))
- input_grad: bfloat16 [32768, 768], P(('shard', 'rep'))
- grad_w_query: float32 [768, 768], P('shard')
- grad_w_key: float32 [768, 768], P('shard')
- grad_w_value: float32 [768, 768], P('shard')
- grad_w_output: float32 [768, 768], P('shard')
- grad_w_router: float32 [768, 8], P('shard')
- grad_gain_attn: float32 [768], P('shard')
- grad_gain_expert: float32 [768], P('shard')
- grad_rel_bias: float32 [32, 12], P('shard')
- grad_w_in: float32 [8, 768, 3072], P('shard', None, 'rep')
- grad_w_out: float32 [8, 3072, 768], P('shard', 'rep')
The draws below stay inside these ranges and needn't reach their ends.
Inputs may be any that keep to these rules, and one draw needn't show every extreme that they name: `segment_ids`: document numbers never fall along a sequence. `expert_ids`: a token's two experts differ; among the tokens of one device no expert is named more than 384 times, a bound that some block reaches.
All inputs are finite; a program needn't handle non-finite values.
Results may differ from the reference program's by a relative error of at most 0.02.
Values may be sent and summed in bfloat16 or wider, within the bound.
No kernel may reach another device: no remote copies, remote signals or barrier semaphores. Data moves between devices by JAX's collectives and lax.ppermute only.
A program may use at most 320 MiB of HBM per device.

```python
import math
import jax
import jax.numpy as jnp
import numpy as np
from jax import lax

D = 768
HEADS = 12
HEAD_DIM = 64
FF = 3072
SEQ_LEN = 1024
BUCKETS = 32
MAX_DISTANCE = 128
DOCS = 4
TOK_DEV = 1024
SEQS = 32
TOKENS = 32768
EXPERTS = 8
CAP = 384
N_SHARD = 8
N_REP = 4


def steps_of(own_key, shape, shards, low, largest):
    level = 1.0
    for position, parts in shards:
        heights = jax.random.uniform(jax.random.fold_in(jax.random.fold_in(own_key, 6), position), (parts,), jnp.float32, low / len(shards), largest / len(shards))
        level = level * jnp.repeat(jnp.exp(heights), shape[position] // parts).reshape((-1,) + (1,) * (len(shape) - 1 - position))
    return level


def length_profile(count, total, most, lean):
    loads = [(1 << 20) // math.isqrt(grade ** lean) + 1 for grade in range(2, count + 1)]
    spare, counts = total - most - (count - 1), [1] * (count - 1)
    while spare > 0:
        movable = [i for i in range(count - 1) if counts[i] < most]
        mass, remaining = sum([loads[i] for i in movable]), spare
        for i in movable:
            more = min(most - counts[i], max(1, remaining * loads[i] // mass), spare)
            counts[i] = counts[i] + more
            spare = spare - more
    return np.array([most] + counts)


def uneven_parts(rng, amount, total, reach, slope):
    if amount == 2:
        one = jax.random.randint(rng, (), max(1, total - reach), min(reach, total - 1) + 1)
        return jnp.stack([one, total - one])
    tallies = jnp.asarray(length_profile(amount, total, reach, slope), jnp.int32)
    couples = (amount - 1) // 2
    source_of, sink = tallies[1:1 + 2 * couples:2], tallies[2:2 + 2 * couples:2]
    slack = jnp.minimum(source_of - 1, reach - sink)
    shifted = jax.random.randint(jax.random.fold_in(rng, 1), (couples,), 0, 1 << 20) % (slack + 1)
    tallies = tallies.at[1:1 + 2 * couples:2].set(source_of - shifted).at[2:2 + 2 * couples:2].set(sink + shifted)
    return tallies[jax.random.permutation(jax.random.fold_in(rng, 2), amount)]


def deal_out(own_key, own, number, rows, number_of, top, most, skew):
    sequence = jax.random.permutation(own_key, number_of)
    crowded, common = load_shares(number_of, rows * top, most, skew, True), load_shares(number_of, rows * top, most, skew, False)
    places = jnp.arange(number_of)

    def named(sizes, rotation):
        used = int((sizes > 0).sum())
        fixed = max(1, used // 4)
        shifted = fixed + (places - fixed + rotation * (used - fixed)) % max(1, number_of - fixed)
        return jnp.zeros((number_of,), jnp.int32).at[sequence[jnp.where(places < fixed, places, shifted)]].set(jnp.asarray(sizes, jnp.int32))

    sizes = jnp.where(number % 4 == 0, named(crowded, number // 4), named(common, number - number // 4 - 1))
    mixed = jax.random.permutation(jax.random.fold_in(own, 3), number_of)
    donor, taker = mixed[0:number_of // 2 * 2:2], mixed[1:number_of // 2 * 2:2]
    room = jnp.minimum(sizes[donor] - 1, most - sizes[taker]) // 2
    room = jnp.where((donor == sequence[0]) | (taker == sequence[0]) | (sizes[taker] == 0), 0, jnp.maximum(room, 0))
    shifted = jax.random.randint(jax.random.fold_in(own, 4), (number_of // 2,), 0, 1 << 20) % (room + 1)
    sizes = sizes.at[donor].add(-shifted).at[taker].add(shifted)
    items = jnp.searchsorted(jnp.cumsum(sizes), jnp.arange(rows * top), side="right").astype(jnp.int32)
    table = items.reshape(top, rows).T
    table = table[jax.random.permutation(jax.random.fold_in(own, 1), rows)]
    rotation = jax.random.randint(jax.random.fold_in(own, 2), (rows, 1), 0, top)
    return jnp.take_along_axis(table, (jnp.arange(top)[None, :] + rotation) % top, axis=1)


def load_shares(count, total, limit, slope, full):
    portions = [(1 << 20) // math.isqrt(rank ** slope) + 1 for rank in range(1, count + 1)]
    largest = limit if full else min(limit, max(-(-total // count), total * portions[0] // sum(portions)))
    least = 1 if total - largest >= count - 1 else 0
    given, surplus = [largest] + [least] * (count - 1), total - largest - least * (count - 1)
    while surplus > 0:
        movable = [i for i in range(1, count) if given[i] < largest] or [i for i in range(1, count) if given[i] < limit]
        pool, left = sum([portions[i] for i in movable]), surplus
        for i in movable:
            more = min(limit - given[i], max(1, left * portions[i] // pool), surplus)
            given[i] = given[i] + more
            surplus = surplus - more
    return np.array(given)


def centred(stream_key, dims, scale, limit, split=(), kind=jnp.bfloat16):
    values = jax.random.normal(stream_key, dims, jnp.float32) * scale
    if len(split) > 0:
        values = steps_of(stream_key, dims, split, -0.22, 0.18) * values
    return jnp.clip(values, min=-limit, max=limit).astype(kind)


def setup_inputs(seed: int = 0) -> dict:
    streams_of = jax.random.split(jax.random.key(seed), 15)
    inputs = centred(streams_of[0], (TOKENS, D), 1.0, 6.0, ((0, 32),))
    w_query = centred(streams_of[1], (D, D), D ** -0.5, 0.21875, ((0, 8),))
    w_key = centred(streams_of[2], (D, D), D ** -0.5, 0.21875, ((0, 8),))
    w_value = centred(streams_of[3], (D, D), D ** -0.5, 0.21875, ((0, 8),))
    w_output = centred(streams_of[4], (D, D), (D // 16) ** -0.5, 0.875, ((0, 8),))
    w_router = centred(streams_of[5], (D, EXPERTS), (2 * D) ** -0.5, 0.15625, ((0, 8),))
    gain_attn = jnp.clip(1.0 + 0.1 * jax.random.normal(streams_of[6], (D,), jnp.float32), 0.5, 1.5).astype(jnp.bfloat16)
    gain_expert = jnp.clip(1.0 + 0.1 * jax.random.normal(streams_of[7], (D,), jnp.float32), 0.5, 1.5).astype(jnp.bfloat16)
    rel_bias = centred(streams_of[8], (BUCKETS, HEADS), 1.0, 4.0, ((0, 8),))
    w_in = centred(streams_of[9], (EXPERTS, D, FF), D ** -0.5, 0.21875, ((0, 8),))
    w_out = centred(streams_of[10], (EXPERTS, FF, D), (FF // 4) ** -0.5, 0.21875, ((0, 8),))
    segment_ids = jax.vmap(lambda own: jnp.searchsorted(jnp.cumsum(uneven_parts(own, DOCS, SEQ_LEN, SEQ_LEN // 2, 0)), jnp.arange(SEQ_LEN), side="right"))(jax.random.split(streams_of[11], SEQS)).reshape((SEQS, SEQ_LEN)).astype(jnp.int32)
    expert_ids_keys = jax.random.split(jax.random.fold_in(streams_of[12], 1), TOKENS // TOK_DEV)
    expert_ids_turns = jax.random.permutation(jax.random.fold_in(streams_of[12], 3), TOKENS // TOK_DEV)
    expert_ids = jax.vmap(lambda own, number: deal_out(jax.random.fold_in(streams_of[12], 2), own, number, TOK_DEV, EXPERTS, 2, CAP, 1))(expert_ids_keys, expert_ids_turns).reshape((TOKENS, 2))
    out_grad = centred(streams_of[13], (TOKENS, D), 1.0, 6.0, ((0, 32),))
    return dict(inputs=inputs, w_query=w_query, w_key=w_key, w_value=w_value, w_output=w_output, w_router=w_router, gain_attn=gain_attn, gain_expert=gain_expert, rel_bias=rel_bias, w_in=w_in, w_out=w_out, segment_ids=segment_ids, expert_ids=expert_ids, out_grad=out_grad)


@jax.custom_vjp
def low(v):
    return lax.optimization_barrier(v.astype(jnp.bfloat16)).astype(jnp.float32)

@jax.custom_vjp
def low_back(v):
    return v

def low_keep(v):
    return (low(v), None)

def low_pass(kept, grad):
    return (grad,)

def backward_kept_mask(v):
    return (v, None)

def back_low(kept, grad):
    return (low(grad),)
low.defvjp(low_keep, low_pass)
low_back.defvjp(backward_kept_mask, back_low)
eps_norm = 1e-06
neg_fill = -1000000000.0

def rms_scale(values, gain_vec):
    mean_square = lax.optimization_barrier(jnp.mean(values * values, axis=-1, keepdims=True))
    return values * lax.rsqrt(mean_square + eps_norm) * gain_vec

def bucket_table(distance):
    half_count = BUCKETS // 2
    clipped = jnp.maximum(distance, 0)
    counted = jnp.zeros(distance.shape, jnp.int32)
    for section_number in range(1, half_count):
        threshold = math.ceil(half_count * (MAX_DISTANCE / half_count) ** (section_number / half_count))
        counted = counted + (clipped >= threshold).astype(jnp.int32)
    return jnp.where(clipped < half_count, clipped, half_count + counted)

def exact_dot(left, right):
    return jnp.dot(left, right, precision=lax.Precision.HIGHEST, preferred_element_type=jnp.float32)

def sequence_attention(query_seq, key_seq, value_seq, segment_seq, relative_bias_matrix):
    length = query_seq.shape[0]
    positions = jnp.arange(length, dtype=jnp.int32)
    distance = positions[:, None] - positions[None, :]
    buckets = bucket_table(distance)
    allowed = (distance >= 0) & (segment_seq[:, None] == segment_seq[None, :])
    bias_entries = jnp.transpose(relative_bias_matrix[buckets], (2, 0, 1))
    query_heads = query_seq.reshape(length, HEADS, HEAD_DIM)
    key_heads = key_seq.reshape(length, HEADS, HEAD_DIM)
    head_values = value_seq.reshape(length, HEADS, HEAD_DIM)
    raw_scores = jnp.einsum('qhe,khe->hqk', query_heads, key_heads, precision=lax.Precision.HIGHEST) * HEAD_DIM ** (-0.5)
    scores = low_back(jnp.where(allowed[None], raw_scores + bias_entries, neg_fill))
    attn_probs = low(jax.nn.softmax(scores, axis=-1))
    mixed_rows = jnp.einsum('hqk,khe->qhe', attn_probs, head_values, precision=lax.Precision.HIGHEST)
    return mixed_rows.reshape(length, D)

def expert_apply(packed):
    rows_in, first_weight, second_weight = packed
    pre_act = low_back(exact_dot(rows_in, first_weight))
    active = low(jax.nn.gelu(pre_act, approximate=True))
    return low_back(low(exact_dot(active, second_weight)))

def layer_forward(inputs, w_query, w_key, w_value, w_output, w_router, gain_attn, gain_expert, rel_bias, w_in, w_out, segment_ids, expert_ids, route_rows):
    normed = low(rms_scale(inputs, gain_attn))
    queries = low_back(low(exact_dot(normed, w_query)))
    key_rows = low_back(low(exact_dot(normed, w_key)))
    value_rows = low_back(low(exact_dot(normed, w_value)))
    group_size = math.gcd(SEQS, 4)
    count_of_groups = SEQS // group_size
    shaped = (count_of_groups, group_size, SEQ_LEN, D)

    def attend_group(pieces):
        query_grp, key_grp, value_grp, segment_grp = pieces
        return jax.vmap(sequence_attention, in_axes=(0, 0, 0, 0, None))(query_grp, key_grp, value_grp, segment_grp, rel_bias)
    mixed_all = lax.map(jax.checkpoint(attend_group), (queries.reshape(shaped), key_rows.reshape(shaped), value_rows.reshape(shaped), segment_ids.reshape(count_of_groups, group_size, SEQ_LEN)))
    attended = low_back(low(mixed_all.reshape(TOKENS, D)))
    branch = low_back(exact_dot(attended, w_output))
    hidden = inputs + branch
    normed_two = low(rms_scale(hidden, gain_expert))
    logits = exact_dot(normed_two, w_router)
    chosen = jnp.take_along_axis(logits, expert_ids, axis=1)
    gate_probs = jax.nn.softmax(chosen, axis=-1)
    copies = low_back(jnp.broadcast_to(normed_two[:, None, :], (TOKENS, 2, D))).reshape(TOKENS * 2, D)
    flat_experts = expert_ids.reshape(-1)
    flat_rows = route_rows.reshape(-1)
    buffers = jnp.zeros((EXPERTS, N_SHARD * N_REP * CAP, D), jnp.float32).at[flat_experts, flat_rows].set(copies)
    returned = lax.map(jax.checkpoint(expert_apply), (buffers, w_in, w_out))
    routed = returned[flat_experts, flat_rows].reshape(TOKENS, 2, D)
    combined = lax.optimization_barrier(jnp.sum(gate_probs[:, :, None] * routed, axis=1))
    return hidden + combined

def reference(inputs, w_query, w_key, w_value, w_output, w_router, gain_attn, gain_expert, rel_bias, w_in, w_out, segment_ids, expert_ids, out_grad):
    blocks = expert_ids.reshape(N_SHARD * N_REP, TOK_DEV * 2)
    one_hot_matrix = (blocks[:, :, None] == jnp.arange(EXPERTS, dtype=jnp.int32)[None, None, :]).astype(jnp.int32)
    before = jnp.cumsum(one_hot_matrix, axis=1, dtype=jnp.int32) - one_hot_matrix
    slot_ids = lax.optimization_barrier(jnp.sum(before * one_hot_matrix, axis=2, dtype=jnp.int32))
    route_rows = (slot_ids + jnp.arange(N_SHARD * N_REP, dtype=jnp.int32)[:, None] * CAP).reshape(TOKENS, 2)
    floats = tuple((array_in.astype(jnp.float32) for array_in in (inputs, w_query, w_key, w_value, w_output, w_router, gain_attn, gain_expert, rel_bias, w_in, w_out)))

    def forward(inputs_f, query_f, key_f, value_f, output_f, router_f, gain_one, gain_two, table_f, in_f, out_f):
        return layer_forward(inputs_f, query_f, key_f, value_f, output_f, router_f, gain_one, gain_two, table_f, in_f, out_f, segment_ids, expert_ids, route_rows)
    result, pullback = jax.vjp(forward, *floats)
    gradient_list = pullback(out_grad.astype(jnp.float32))
    return (result.astype(jnp.bfloat16), gradient_list[0].astype(jnp.bfloat16), gradient_list[1], gradient_list[2], gradient_list[3], gradient_list[4], gradient_list[5], gradient_list[6], gradient_list[7], gradient_list[8], gradient_list[9], gradient_list[10])
```

```python
import functools
import math
import jax
import jax.numpy as jnp
from jax import lax
from jax.experimental import pallas as pl
from jax.experimental.pallas import tpu as pltpu
from jax.sharding import PartitionSpec as P

HEADS = 12
BUCKETS = 32
MAX_DISTANCE = 128
LONGEST = 512
QB = 256
BIG = 1e9
LANES = 128
FF_TILE = 512
ROW_BLOCK = 384
TILE = 256
CHUNKS = 2
GELU_A = math.sqrt(2 / math.pi)
GELU_B = 0.044715
eps_norm = 1e-06


def bucket_table(distance):
    half_count = BUCKETS // 2
    clipped = jnp.maximum(distance, 0)
    counted = jnp.zeros(distance.shape, jnp.int32)
    for section_number in range(1, half_count):
        threshold = math.ceil(
            half_count * (MAX_DISTANCE / half_count) ** (section_number / half_count)
        )
        counted = counted + (clipped >= threshold).astype(jnp.int32)
    return jnp.where(clipped < half_count, clipped, half_count + counted)


def window_distance():
    span = LONGEST + 2 * QB
    place = jnp.arange(span, dtype=jnp.int32)
    place = jnp.where(place >= LONGEST + QB, place - span, place)
    return LONGEST - place


def bias_rows(table):
    distance = window_distance()
    onehot = bucket_table(distance)[None, :] == jnp.arange(BUCKETS, dtype=jnp.int32)[:, None]
    rows = jnp.sum(
        jnp.where(onehot[None], table.astype(jnp.float32).T[:, :, None], 0.0), axis=1
    )
    return jnp.where(distance[None, :] >= 0, rows, -BIG)


def segment_lanes(segment, width):
    lane = jnp.arange(width, dtype=jnp.int32)[None, :] % (width // 2)
    same = segment[:, None] == lane
    first = lane < 4
    query_lanes = jnp.where(first & same, 1.0, 0.0)
    key_lanes = jnp.where(first, jnp.where(same, 0.0, -BIG), jnp.where(lane < 7, 1.0, 0.0))
    return query_lanes.astype(jnp.bfloat16), key_lanes.astype(jnp.bfloat16)


def toeplitz(row):
    span = row.shape[-1]
    full = jnp.broadcast_to(row, (QB, span))
    return pltpu.roll(full, 0, 1, stride=1, stride_axis=0)[:, : LONGEST + QB]


def nt(a, b):
    return lax.dot_general(a, b, (((1,), (1,)), ((), ())), preferred_element_type=jnp.float32)


def nn(a, b):
    return jnp.dot(a, b, preferred_element_type=jnp.float32)


def tn(a, b):
    return lax.dot_general(a, b, (((0,), (0,)), ((), ())), preferred_element_type=jnp.float32)


def forward_kernel(q_ref, k_ref, v_ref, ql_ref, kl_ref, row_ref, out_ref, lse_ref):
    pair = pl.program_id(0)
    length, width = q_ref.shape
    half = width // 2
    lane = lax.broadcasted_iota(jnp.int32, (QB, width), 1)
    lane_k = lax.broadcasted_iota(jnp.int32, (length, width), 1)

    @pl.when(pair == 0)
    def _():
        lse_ref[...] = jnp.zeros_like(lse_ref)

    biases = [toeplitz(row_ref[0, h : h + 1, :]) for h in range(2)]
    keys = [
        jnp.where((lane_k < half) == (h == 0), k_ref[...], kl_ref[...]) for h in range(2)
    ]
    for start in range(0, length, QB):
        low = max(0, start - LONGEST)
        wide = start + QB - low
        q = (q_ref[start : start + QB, :].astype(jnp.float32) * (half**-0.5)).astype(jnp.bfloat16)
        outs = []
        lse = lse_ref[start : start + QB, :]
        for h in range(2):
            mine = (lane < half) == (h == 0)
            q_own = jnp.where(mine, q, ql_ref[start : start + QB, :])
            s = nt(q_own, keys[h][low : start + QB, :]) + biases[h][:, LONGEST + QB - wide :]
            peak = jnp.max(s, axis=1, keepdims=True)
            p = jnp.exp(s - peak)
            total = jnp.sum(p, axis=1, keepdims=True)
            o = nn(p.astype(jnp.bfloat16), v_ref[low : start + QB, :])
            outs.append(o * (1.0 / total))
            lse = jnp.where(lane == 2 * pair + h, peak + jnp.log(total), lse)
        lse_ref[start : start + QB, :] = lse
        out_ref[start : start + QB, :] = jnp.where(lane < half, outs[0], outs[1]).astype(
            jnp.bfloat16
        )


def attention_forward(qk, v, query_lanes, key_lanes, rows):
    length, model = v.shape
    pairs = HEADS // 2
    width = model // pairs
    span = rows.shape[-1]
    return pl.pallas_call(
        forward_kernel,
        grid=(pairs,),
        in_specs=[
            pl.BlockSpec((length, width), lambda p: (0, p)),
            pl.BlockSpec((length, width), lambda p: (0, p + pairs)),
            pl.BlockSpec((length, width), lambda p: (0, p)),
            pl.BlockSpec((length, width), lambda p: (0, 0)),
            pl.BlockSpec((length, width), lambda p: (0, 0)),
            pl.BlockSpec((1, 2, span), lambda p: (p, 0, 0)),
        ],
        out_specs=[
            pl.BlockSpec((length, width), lambda p: (0, p)),
            pl.BlockSpec((length, width), lambda p: (0, 0)),
        ],
        out_shape=[
            jax.ShapeDtypeStruct((length, model), jnp.bfloat16),
            jax.ShapeDtypeStruct((length, width), jnp.float32),
        ],
        compiler_params=pltpu.CompilerParams(
            dimension_semantics=("arbitrary",), vmem_limit_bytes=40 * 1024 * 1024
        ),
        cost_estimate=pl.CostEstimate(
            flops=1024, bytes_accessed=1024, transcendentals=0
        ),
        name="attention_forward",
    )(qk, qk, v, query_lanes, key_lanes, rows.reshape(pairs, 2, span))


def three_parts(column):
    first = column.astype(jnp.bfloat16).astype(jnp.float32)
    rest = column - first
    second = rest.astype(jnp.bfloat16).astype(jnp.float32)
    return first, second, rest - second


def with_column(lane, half, base, column):
    a, b, c = three_parts(column)
    spare = lane % half
    packed = jnp.where(spare == 4, a, jnp.where(spare == 5, b, jnp.where(spare == 6, c, base)))
    return packed.astype(jnp.bfloat16)


def backward_kernel(
    q_ref, k_ref, v_ref, o_ref, g_ref, ql_ref, kl_ref, row_ref, lse_ref,
    grad_ref, table_ref, dk_acc, dv_acc, diag_acc,
):
    pair = pl.program_id(0)
    length, width = q_ref.shape
    half = width // 2
    window = LONGEST + QB
    lane = lax.broadcasted_iota(jnp.int32, (QB, width), 1)
    lane_k = lax.broadcasted_iota(jnp.int32, (length, width), 1)
    dk_acc[...] = jnp.zeros_like(dk_acc)
    dv_acc[...] = jnp.zeros_like(dv_acc)
    diag_acc[...] = jnp.zeros_like(diag_acc)
    zero = jnp.zeros((), jnp.bfloat16)
    biases = [toeplitz(row_ref[0, h : h + 1, :]).T for h in range(2)]
    owned_k = [(lane_k < half) == (h == 0) for h in range(2)]
    keys = [jnp.where(owned_k[h], k_ref[...], kl_ref[...]) for h in range(2)]
    bare_keys = [jnp.where(owned_k[h], k_ref[...], zero) for h in range(2)]
    values = [jnp.where(owned_k[h], v_ref[...], kl_ref[...]) for h in range(2)]
    for start in range(0, length, QB):
        low = max(0, start - LONGEST)
        wide = start + QB - low
        stop = start + QB
        q = (q_ref[start:stop, :].astype(jnp.float32) * (half**-0.5)).astype(jnp.bfloat16)
        g = g_ref[start:stop, :]
        dot_all = g.astype(jnp.float32) * o_ref[start:stop, :].astype(jnp.float32)
        lse_all = lse_ref[start:stop, :]
        q_lanes = ql_ref[start:stop, :].astype(jnp.float32)
        turned = None
        for h in range(2):
            mine = (lane < half) == (h == 0)
            lse = jnp.sum(jnp.where(lane == 2 * pair + h, lse_all, 0.0), axis=1, keepdims=True)
            dot = jnp.sum(jnp.where(mine, dot_all, 0.0), axis=1, keepdims=True)
            q_own = jnp.where(mine, q, with_column(lane, half, q_lanes, -lse))
            g_own = jnp.where(mine, g, with_column(lane, half, jnp.zeros_like(q_lanes), -dot))
            s = nt(keys[h][low:stop, :], q_own) + biases[h][window - wide :, :]
            p = jnp.exp(s)
            dp = nt(values[h][low:stop, :], g_own)
            ds = p * dp
            diag_acc[h, window - wide :, :] += ds
            ds_low = ds.astype(jnp.bfloat16)
            dv_acc[low:stop, :] += nn(p.astype(jnp.bfloat16), jnp.where(mine, g, zero))
            dk_acc[low:stop, :] += nn(ds_low, jnp.where(mine, q, zero))
            part = tn(bare_keys[h][low:stop, :], ds_low)
            turned = part if turned is None else turned + part
        grad_ref[0, start:stop, :] = (turned * (half**-0.5)).T.astype(jnp.bfloat16)
    grad_ref[1] = dk_acc[...].astype(jnp.bfloat16)
    grad_ref[2] = dv_acc[...].astype(jnp.bfloat16)
    span = window + QB
    for h in range(2):
        flat = jnp.concatenate([diag_acc[h].T, jnp.zeros((QB, QB), jnp.float32)], axis=1)
        eight = flat[0:8, :]
        for row in range(8, QB, 8):
            eight = eight + pltpu.roll(flat[row : row + 8, :], span - row, 1)
        total = eight[0:1, :]
        for row in range(1, 8):
            total = total + pltpu.roll(eight[row : row + 1, :], span - row, 1)
        table_ref[0, h : h + 1, :] = total


def attention_backward(qk, v, attended, grad_attended, query_lanes, key_lanes, rows, lse):
    length, model = v.shape
    pairs = HEADS // 2
    width = model // pairs
    span = rows.shape[-1]
    block = pl.BlockSpec((length, width), lambda p: (0, p))
    same = pl.BlockSpec((length, width), lambda p: (0, 0))
    low = jax.ShapeDtypeStruct((3, length, model), jnp.bfloat16)
    return pl.pallas_call(
        backward_kernel,
        grid=(pairs,),
        in_specs=[
            block,
            pl.BlockSpec((length, width), lambda p: (0, p + pairs)),
            pl.BlockSpec((length, width), lambda p: (0, p)),
            block,
            block,
            same,
            same,
            pl.BlockSpec((1, 2, span), lambda p: (p, 0, 0)),
            same,
        ],
        out_specs=[
            pl.BlockSpec((3, length, width), lambda p: (0, 0, p)),
            pl.BlockSpec((1, 2, span), lambda p: (p, 0, 0)),
        ],
        out_shape=[low, jax.ShapeDtypeStruct((pairs, 2, span), jnp.float32)],
        scratch_shapes=[
            pltpu.VMEM((length, width), jnp.float32),
            pltpu.VMEM((length, width), jnp.float32),
            pltpu.VMEM((2, LONGEST + QB, QB), jnp.float32),
        ],
        compiler_params=pltpu.CompilerParams(
            dimension_semantics=("arbitrary",), vmem_limit_bytes=48 * 1024 * 1024
        ),
        cost_estimate=pl.CostEstimate(
            flops=1024, bytes_accessed=1024, transcendentals=0
        ),
        name="attention_backward",
    )(
        qk, qk, v, attended, grad_attended, query_lanes, key_lanes,
        rows.reshape(pairs, 2, span), lse,
    )


def table_gradient(diagonals):
    distance = window_distance()
    onehot = (bucket_table(distance)[:, None] == jnp.arange(BUCKETS, dtype=jnp.int32)[None, :]) & (
        distance >= 0
    )[:, None]
    flat = diagonals.reshape(HEADS, -1)
    return jnp.sum(jnp.where(onehot[:, :, None], flat.T[:, None, :], 0.0), axis=0)


def expert_forward_kernel(
    me_ref, x_ref, g_ref, sum_ref, in_ref, out_ref, router_ref, *refs
):
    y_ref, active_ref, gated_ref, slope_ref, logit_ref, router_grad_ref = refs[-6:]
    step = pl.program_id(0)
    model, hidden = in_ref.shape
    rows = x_ref.shape[0] * x_ref.shape[1]
    x = x_ref[...].reshape(rows, model)
    grad = g_ref[...].reshape(rows, model).astype(jnp.float32)
    id_sum = sum_ref[...].reshape(rows, LANES).astype(jnp.float32)
    me = me_ref[0].astype(jnp.float32)
    lane = lax.broadcasted_iota(jnp.int32, (rows, LANES), 1)
    expert = (lane % (LANES // 2)).astype(jnp.float32)
    own = expert == me
    other = expert == id_sum - me
    first = lane < LANES // 2
    logits = nn(x, router_ref[...])
    own_logit = jnp.sum(jnp.where(first & own, logits, 0.0), axis=1, keepdims=True)
    other_logit = jnp.sum(jnp.where(first & other, logits, 0.0), axis=1, keepdims=True)
    gate = 1.0 / (1.0 + jnp.exp(other_logit - own_logit))
    other_gate = 1.0 / (1.0 + jnp.exp(own_logit - other_logit))
    gated_ref[...] = (gate * grad).astype(jnp.bfloat16)
    for low in range(0, hidden, FF_TILE):
        cut = slice(low, low + FF_TILE)
        v = nn(x, in_ref[:, cut])
        square = v * v
        t = jnp.tanh(v * (GELU_A + GELU_A * GELU_B * square))
        h = 0.5 + 0.5 * t
        a = v * h
        slope = h + (a * (1.0 - h)) * (2.0 * GELU_A + 6.0 * GELU_A * GELU_B * square)
        active_ref[:, cut] = a.astype(jnp.bfloat16)
        slope_ref[:, cut] = slope.astype(jnp.bfloat16)
    result = nn(active_ref[...], out_ref[...])
    y_ref[...] = (gate * result).astype(jnp.bfloat16).reshape(y_ref.shape)
    gate_grad = jnp.sum(grad * result, axis=1, keepdims=True)
    weight = gate * other_gate * gate_grad
    logit_grad = jnp.where(own, weight, 0.0) - jnp.where(other, weight, 0.0)
    high = logit_grad.astype(jnp.bfloat16)
    rest = (logit_grad - high.astype(jnp.float32)).astype(jnp.bfloat16)
    logit_low = jnp.where(first, high, rest)
    logit_ref[...] = logit_low
    part = tn(x, logit_low)

    @pl.when(step == 0)
    def _():
        router_grad_ref[...] = part

    @pl.when(step > 0)
    def _():
        router_grad_ref[...] += part


def expert_backward_kernel(
    gated_ref, slope_ref, logit_ref, in_ref, out_ref, router_ref, *refs
):
    pre_ref, back_ref = refs[-2:]
    hidden = in_ref.shape[1]
    gated = gated_ref[...]
    for low in range(0, hidden, FF_TILE):
        cut = slice(low, low + FF_TILE)
        d = nt(gated, out_ref[cut, :])
        pre_ref[:, cut] = (d * slope_ref[:, cut].astype(jnp.float32)).astype(jnp.bfloat16)
    back = nt(pre_ref[...], in_ref[...]) + nt(logit_ref[...], router_ref[...])
    back_ref[...] = back.astype(jnp.bfloat16).reshape(back_ref.shape)


def low_shape(*dims):
    return jax.ShapeDtypeStruct(dims, jnp.bfloat16)


def expert_forward(me, x, grads, sums, chunk, weight_in, weight_out, router_two, kept):
    experts, half, model = x.shape
    hidden = weight_in.shape[1]
    group = max(1, min(experts, ROW_BLOCK // half))
    rows = group * half
    total = experts * half
    fixed = lambda *dims: pl.BlockSpec(dims, lambda i, m: (0, 0), pipeline_mode=pl.Buffered(1))
    flat = lambda width: pl.BlockSpec((rows, width), lambda i, m: (i, 0))
    steps = experts // group
    joint = lambda width: pl.BlockSpec((rows, width), lambda i, m: (i + chunk * steps, 0))
    return pl.pallas_call(
        expert_forward_kernel,
        grid_spec=pltpu.PrefetchScalarGridSpec(
            num_scalar_prefetch=1,
            grid=(experts // group,),
            in_specs=[
                pl.BlockSpec((group, half, model), lambda i, m: (i, 0, 0)),
                pl.BlockSpec((group, half, model), lambda i, m: (i, chunk, 0)),
                pl.BlockSpec((group, half, LANES), lambda i, m: (i, chunk, 0)),
                fixed(model, hidden),
                fixed(hidden, model),
                fixed(model, LANES),
            ]
            + [pl.BlockSpec(memory_space=pl.ANY)] * len(kept),
            out_specs=[
                pl.BlockSpec((group, half, model), lambda i, m: (i, chunk, 0)),
                joint(hidden),
                joint(model),
                flat(hidden),
                flat(LANES),
                pl.BlockSpec((model, LANES), lambda i, m: (0, 0)),
            ],
        ),
        out_shape=[
            low_shape(experts, CHUNKS * half, model),
            low_shape(CHUNKS * total, hidden),
            low_shape(CHUNKS * total, model),
            low_shape(total, hidden),
            low_shape(total, LANES),
            jax.ShapeDtypeStruct((model, LANES), jnp.float32),
        ],
        compiler_params=pltpu.CompilerParams(
            dimension_semantics=("arbitrary",), vmem_limit_bytes=56 * 1024 * 1024
        ),
        cost_estimate=pl.CostEstimate(
            flops=4 * total * model * hidden,
            bytes_accessed=4 * total * hidden + 4 * model * hidden + 8 * total * model,
            transcendentals=total * hidden,
        ),
        input_output_aliases={7 + place: place for place in range(len(kept))},
        name="expert_forward",
    )(me, x, grads, sums, weight_in, weight_out, router_two, *kept)


def expert_backward(
    experts, gated, slope, logit_low, chunk, weight_in, weight_out, router_two, kept
):
    total, hidden = slope.shape
    model = gated.shape[1]
    half = total // experts
    group = max(1, min(experts, ROW_BLOCK // half))
    rows = group * half
    fixed = lambda *dims: pl.BlockSpec(dims, lambda i: (0, 0), pipeline_mode=pl.Buffered(1))
    flat = lambda width: pl.BlockSpec((rows, width), lambda i: (i, 0))
    steps = experts // group
    joint = lambda width: pl.BlockSpec((rows, width), lambda i: (i + chunk * steps, 0))
    return pl.pallas_call(
        expert_backward_kernel,
        grid=(experts // group,),
        in_specs=[
            joint(model),
            flat(hidden),
            flat(LANES),
            fixed(model, hidden),
            fixed(hidden, model),
            fixed(model, LANES),
        ]
        + [pl.BlockSpec(memory_space=pl.ANY)] * len(kept),
        out_specs=[joint(hidden), pl.BlockSpec((group, half, model), lambda i: (i, 0, 0))],
        out_shape=[low_shape(CHUNKS * total, hidden), low_shape(experts, half, model)],
        compiler_params=pltpu.CompilerParams(
            dimension_semantics=("arbitrary",), vmem_limit_bytes=56 * 1024 * 1024
        ),
        cost_estimate=pl.CostEstimate(flops=1024, bytes_accessed=1024, transcendentals=0),
        input_output_aliases={6 + place: place for place in range(len(kept))},
        name="expert_backward",
    )(gated, slope, logit_low, weight_in, weight_out, router_two, *kept)


def swap(values, axis, bit):
    count = lax.axis_size(axis)
    return lax.ppermute(values, axis, [(place, place ^ bit) for place in range(count)])


def bits_of(axis):
    count = lax.axis_size(axis)
    return [1 << place for place in range(count.bit_length() - 1)]


def spread_rows(part, axis, bits):
    held, offsets = part[None], [0]
    for bit in bits:
        held = jnp.concatenate([held, swap(held, axis, bit)], axis=0)
        offsets = offsets + [offset ^ bit for offset in offsets]
    place = [0] * len(offsets)
    for index, offset in enumerate(offsets):
        place[offset // 2] = index
    return held, swap(held, axis, 1), place


def order_kernel(order_ref, *refs):
    count = len(refs) // 3
    chips = refs[0].shape[0]
    core = order_ref[0]
    for part in range(count):
        near, far, out = refs[2 * part], refs[2 * part + 1], refs[2 * count + part]
        for chip in range(chips):
            source = order_ref[1 + part * chips + chip]
            out[chip, core] = near[source]
            out[chip, 1 - core] = far[source]


def gather_rows(parts, axis, orders):
    spread = [spread_rows(part, axis, bits) for part, bits in zip(parts, orders)]
    me = lax.axis_index(axis).astype(jnp.int32)
    chips = spread[0][0].shape[0]
    order = [(me % 2)[None]]
    for _, _, place in spread:
        order.append(
            jnp.asarray(place, jnp.int32)[jnp.arange(chips, dtype=jnp.int32) ^ (me // 2)]
        )
    whole = pl.BlockSpec(memory_space=pltpu.VMEM)
    full = pl.pallas_call(
        order_kernel,
        in_specs=[pl.BlockSpec(memory_space=pltpu.SMEM)] + [whole] * (2 * len(parts)),
        out_specs=[whole] * len(parts),
        out_shape=[
            jax.ShapeDtypeStruct((chips, 2) + part.shape, part.dtype) for part in parts
        ],
        compiler_params=pltpu.CompilerParams(vmem_limit_bytes=24 * 1024 * 1024),
        name="rows_in_order",
    )(jnp.concatenate(order), *(array for near, far, _ in spread for array in (near, far)))
    return [
        array.reshape(2 * chips * part.shape[0], part.shape[1])
        for array, part in zip(full, parts)
    ], [near for near, _, _ in spread]


def scatter_sum(blocks, axis):
    count, rows, width = blocks.shape
    bits = bits_of(axis)
    me = lax.axis_index(axis)

    def step(values, left, bit):
        at = left.index(bit)
        mine = (me // bit) % 2
        keep = lax.dynamic_index_in_dim(values, mine, at, keepdims=False)
        away = lax.dynamic_index_in_dim(values, 1 - mine, at, keepdims=False)
        came = swap(away, axis, bit)
        total = keep.astype(jnp.float32) + came.astype(jnp.float32)
        return total.astype(jnp.bfloat16), [other for other in left if other != bit]

    left = bits[::-1]
    values = blocks.reshape((2,) * len(bits) + (rows, width))
    values, left = step(values, left, 1)
    cut = width // 2
    parts = []
    for half, order in ((values[..., :cut], bits[1:]), (values[..., cut:], bits[:0:-1])):
        remaining = left
        for bit in order:
            half, remaining = step(half, remaining, bit)
        parts.append(half)
    return jnp.concatenate(parts, axis=-1)


def sum_all(values, axis):
    rows = values.shape[0]
    bits = bits_of(axis)
    mine = lax.axis_index(axis) % 2
    low, high = values[: rows // 2], values[rows // 2 :]
    keep = jnp.where(mine == 0, low, high)
    came = swap(jnp.where(mine == 0, high, low), axis, 1)
    half = (keep.astype(jnp.float32) + came.astype(jnp.float32)).astype(jnp.bfloat16)
    for bit in bits[1:]:
        came = swap(half, axis, bit)
        half = (half.astype(jnp.float32) + came.astype(jnp.float32)).astype(jnp.bfloat16)
    came = swap(half, axis, 1)
    return jnp.concatenate(
        [jnp.where(mine == 0, half, came), jnp.where(mine == 0, came, half)], axis=0
    )


def weight_grad_kernel(steps, left_ref, right_ref, *refs):
    out_ref, turned = refs[-2:]
    step = pl.program_id(0)

    @pl.when(step == 0)
    def _():
        turned[...] = left_ref[...].T

    def product():
        out_ref[...] = nn(turned[...], right_ref[0]).astype(jnp.bfloat16)

    if len(refs) == 2:
        product()
    else:
        pl.when(step < steps)(product)

        @pl.when(step >= steps)
        def _():
            out_ref[...] = refs[0][...]


def weight_grad(left, right, extra=None):
    tokens, model = left.shape
    parts, _, width = right.shape
    cuts = width // TILE
    steps = parts * cuts
    last = steps - 1
    in_specs = [
        pl.BlockSpec((tokens, model), lambda i: (0, 0)),
        pl.BlockSpec(
            (1, tokens, TILE), lambda i: (jnp.minimum(i, last) // cuts, 0, jnp.minimum(i, last) % cuts)
        ),
    ]
    operands = [left, right]
    if extra is not None:
        in_specs.append(pl.BlockSpec((model, TILE), lambda i: (0, jnp.maximum(i - last - 1, 0))))
        operands.append(extra)
        steps = steps + extra.shape[1] // TILE
    return pl.pallas_call(
        functools.partial(weight_grad_kernel, last + 1),
        grid=(steps,),
        in_specs=in_specs,
        out_specs=pl.BlockSpec((model, TILE), lambda i: (0, i)),
        out_shape=jax.ShapeDtypeStruct((model, steps * TILE), jnp.bfloat16),
        scratch_shapes=[pltpu.VMEM((model, tokens), jnp.bfloat16)],
        compiler_params=pltpu.CompilerParams(
            dimension_semantics=("arbitrary",), vmem_limit_bytes=32 * 1024 * 1024
        ),
        cost_estimate=pl.CostEstimate(flops=1024, bytes_accessed=1024, transcendentals=0),
        name="weight_grad",
    )(*operands)


def rms_scale(values, gain_vec):
    mean_square = jnp.mean(values * values, axis=-1, keepdims=True)
    return values * lax.rsqrt(mean_square + eps_norm) * gain_vec


def pick_rows(places, source):
    return jnp.dot(places, source, preferred_element_type=jnp.float32).astype(jnp.bfloat16)


def back_rows(places, slots):
    return jnp.einsum("st,sd->td", places, slots, preferred_element_type=jnp.float32)


def body(
    inputs,
    w_query,
    w_key,
    w_value,
    w_output,
    w_router,
    gain_attn,
    gain_expert,
    rel_bias,
    w_in,
    w_out,
    segment_ids,
    expert_ids,
    out_grad,
):
    tokens_here, model_width = inputs.shape
    experts = lax.axis_size("shard")
    me = lax.axis_index("shard").astype(jnp.int32)
    capacity = 3 * tokens_here // experts
    half = capacity // CHUNKS
    rows_here = w_query.shape[0]
    table_here = rel_bias.shape[0]
    table_at = experts + 2

    small = jnp.concatenate(
        [
            w_router,
            gain_attn[:, None],
            gain_expert[:, None],
            jnp.pad(rel_bias, ((0, rows_here - table_here), (0, 0))),
            jnp.zeros((rows_here, LANES - table_at - HEADS), jnp.bfloat16),
        ],
        axis=1,
    )
    bits = bits_of("shard")
    (first_full, second_full), (first_held, second_held) = gather_rows(
        (
            jnp.concatenate([w_query, w_key, small], axis=1),
            jnp.concatenate([w_value, w_output], axis=1),
        ),
        "shard",
        (bits[1:], bits[:0:-1]),
    )
    qk_full = first_full[:, : 2 * model_width]
    small_full = first_full[:, 2 * model_width :]
    value_full = second_full[:, :model_width]
    output_full = second_full[:, model_width:]
    router_full = small_full[:, :experts]
    gain_one = small_full[:, experts].astype(jnp.float32)
    gain_two = small_full[:, experts + 1].astype(jnp.float32)
    table_full = small_full.reshape(experts, rows_here, LANES)[
        :, :table_here, table_at : table_at + HEADS
    ].reshape(BUCKETS, HEADS)
    router_two = jnp.pad(router_full, ((0, 0), (0, LANES // 2 - experts)))
    router_two = jnp.concatenate([router_two, router_two], axis=1)

    flat_ids = expert_ids.reshape(-1)
    onehot_count = (flat_ids[:, None] == jnp.arange(experts, dtype=jnp.int32)[None, :]).astype(
        jnp.int32
    )
    before = jnp.cumsum(onehot_count, axis=0, dtype=jnp.int32) - onehot_count
    slot_ids = jnp.sum(before * onehot_count, axis=1, dtype=jnp.int32)
    flat_rows = (flat_ids * capacity + slot_ids).reshape(tokens_here, 2)
    def places_of(low, count):
        slots = (
            jnp.arange(experts, dtype=jnp.int32)[:, None] * capacity
            + low
            + jnp.arange(count, dtype=jnp.int32)[None, :]
        ).reshape(-1)
        hit = (slots[:, None] == flat_rows[None, :, 0]) | (slots[:, None] == flat_rows[None, :, 1])
        return hit.astype(jnp.bfloat16)

    places = [places_of(chunk * half, half) for chunk in range(CHUNKS)]
    all_places = places_of(0, capacity)

    id_sum = jnp.sum(expert_ids, axis=1).astype(jnp.float32)
    slot_sums = jnp.dot(all_places.astype(jnp.float32), id_sum).reshape(experts, capacity)
    slot_sums = lax.all_to_all(slot_sums, "shard", split_axis=0, concat_axis=0, tiled=True)
    slot_sums = jnp.broadcast_to(
        slot_sums[:, :, None], (experts, capacity, LANES)
    ).astype(jnp.bfloat16)
    grad_send = pick_rows(all_places, out_grad).reshape(experts, capacity, model_width)
    grad_send, first_held, second_held = lax.optimization_barrier(
        (grad_send, first_held, second_held)
    )
    grad_received = lax.all_to_all(grad_send, "shard", split_axis=0, concat_axis=0, tiled=True)

    inputs_f = inputs.astype(jnp.float32)
    normed = rms_scale(inputs_f, gain_one).astype(jnp.bfloat16)
    qk = jnp.dot(normed, qk_full, preferred_element_type=jnp.float32).astype(jnp.bfloat16)
    value = jnp.dot(normed, value_full, preferred_element_type=jnp.float32).astype(jnp.bfloat16)
    query_lanes, key_lanes = segment_lanes(segment_ids[0], model_width // (HEADS // 2))
    rows = bias_rows(table_full)
    attended, lse = attention_forward(qk, value, query_lanes, key_lanes, rows)
    hidden = inputs_f + jnp.dot(attended, output_full, preferred_element_type=jnp.float32)
    normed_two = rms_scale(hidden, gain_two).astype(jnp.bfloat16)

    normed_two, grad_received = lax.optimization_barrier((normed_two, grad_received))
    weight_in = w_in[0]
    weight_out = w_out[0]
    sent = [
        lax.all_to_all(
            pick_rows(places[k], normed_two).reshape(experts, half, model_width),
            "shard",
            split_axis=0,
            concat_axis=0,
            tiled=True,
        )
        for k in range(CHUNKS)
    ]
    kept = ()
    slopes, logit_lows = [], []
    router_part = jnp.zeros((model_width, LANES), jnp.float32)
    for k in range(CHUNKS):
        *kept, slope, logit_low, part = expert_forward(
            me[None],
            sent[k],
            grad_received,
            slot_sums,
            k,
            weight_in,
            weight_out,
            router_two,
            kept,
        )
        slopes.append(slope)
        logit_lows.append(logit_low)
        router_part = router_part + part
    results, active, gated = kept
    grad_out_part = jnp.einsum(
        "rf,rd->fd", active, gated, preferred_element_type=jnp.float32
    ).astype(jnp.bfloat16)
    out_summed = lax.psum_scatter(grad_out_part, "rep", scatter_dimension=0, tiled=True)
    gated, grad_out_part = lax.optimization_barrier((gated, grad_out_part))
    kept = ()
    returned = []
    for k in range(CHUNKS):
        *kept, back = expert_backward(
            experts,
            gated,
            slopes[k],
            logit_lows[k],
            k,
            weight_in,
            weight_out,
            router_two,
            kept,
        )
        returned.append(
            lax.all_to_all(back, "shard", split_axis=0, concat_axis=0, tiled=True)
        )
    returned[0], grad_pre = lax.optimization_barrier((returned[0], kept[0]))
    rows_in = jnp.concatenate([part.reshape(-1, model_width) for part in sent], axis=0)
    grad_in_part = jnp.einsum(
        "rd,rf->df", rows_in, grad_pre, preferred_element_type=jnp.float32
    ).astype(jnp.bfloat16)
    in_summed = lax.psum_scatter(grad_in_part, "rep", scatter_dimension=1, tiled=True)
    *returned, grad_in_part, results = lax.optimization_barrier(
        (*returned, grad_in_part, results)
    )
    results = lax.all_to_all(results, "shard", split_axis=0, concat_axis=0, tiled=True)

    grad_out = out_grad.astype(jnp.float32)
    grad_normed_two = sum(
        back_rows(places[k], returned[k].reshape(-1, model_width)) for k in range(CHUNKS)
    )
    unused_two, norm_two_pull = jax.vjp(rms_scale, hidden, gain_two)
    grad_hidden_norm, grad_gain_two = norm_two_pull(grad_normed_two)
    grad_hidden = grad_out + grad_hidden_norm
    grad_branch = grad_hidden.astype(jnp.bfloat16)
    grad_wo = weight_grad(attended, grad_branch[None])
    grad_attended = jnp.einsum(
        "te,de->td", grad_branch, output_full, preferred_element_type=jnp.float32
    ).astype(jnp.bfloat16)

    out_summed, grad_attended = lax.optimization_barrier((out_summed, grad_attended))
    grad_qkv, diagonals = attention_backward(
        qk, value, attended, grad_attended, query_lanes, key_lanes, rows, lse
    )
    grad_qkv, results = lax.optimization_barrier((grad_qkv, results))
    grad_table = table_gradient(diagonals)
    grad_normed = jnp.zeros((tokens_here, model_width), jnp.float32)
    for place, weight in enumerate(
        (qk_full[:, :model_width], qk_full[:, model_width:], value_full)
    ):
        grad_normed = grad_normed + jnp.einsum(
            "te,de->td", grad_qkv[place], weight, preferred_element_type=jnp.float32
        )
    unused_one, norm_one_pull = jax.vjp(rms_scale, inputs_f, gain_one)
    grad_inputs_norm, grad_gain_one = norm_one_pull(grad_normed)
    input_grad = (grad_hidden + grad_inputs_norm).astype(jnp.bfloat16)

    grad_router = router_part[:, :experts] + router_part[
        :, LANES // 2 : LANES // 2 + experts
    ]
    table_rows = jnp.pad(
        grad_table.reshape(experts, table_here, HEADS),
        ((0, 0), (0, rows_here - table_here), (0, 0)),
    ).reshape(model_width, HEADS)
    small_grads = jnp.concatenate(
        [
            grad_router,
            grad_gain_one[:, None],
            grad_gain_two[:, None],
            table_rows,
            jnp.zeros((model_width, TILE - table_at - HEADS), jnp.float32),
        ],
        axis=1,
    )
    packed = weight_grad(
        normed,
        grad_qkv,
        jnp.concatenate([grad_wo, small_grads.astype(jnp.bfloat16)], axis=1),
    )
    owned = scatter_sum(packed.reshape(experts, rows_here, packed.shape[1]), "shard")
    owned, in_summed = lax.optimization_barrier((owned, in_summed))
    summed = sum_all(owned, "rep").astype(jnp.float32)
    small_sum = summed[:, 4 * model_width :]

    combined = back_rows(all_places, results.reshape(-1, model_width))
    output = (hidden + combined).astype(jnp.bfloat16)
    return (
        output,
        input_grad,
        summed[:, :model_width],
        summed[:, model_width : 2 * model_width],
        summed[:, 2 * model_width : 3 * model_width],
        summed[:, 3 * model_width : 4 * model_width],
        small_sum[:, :experts],
        small_sum[:, experts],
        small_sum[:, experts + 1],
        small_sum[:table_here, table_at : table_at + HEADS],
        in_summed.astype(jnp.float32)[None],
        out_summed.astype(jnp.float32)[None],
    )


def solution(mesh):
    in_specs = (
        P(("shard", "rep"), None),
        P("shard", None),
        P("shard", None),
        P("shard", None),
        P("shard", None),
        P("shard", None),
        P("shard"),
        P("shard"),
        P("shard", None),
        P("shard", None, None),
        P("shard", None, None),
        P(("shard", "rep"), None),
        P(("shard", "rep"), None),
        P(("shard", "rep"), None),
    )
    out_specs = (
        P(("shard", "rep"), None),
        P(("shard", "rep"), None),
        P("shard", None),
        P("shard", None),
        P("shard", None),
        P("shard", None),
        P("shard", None),
        P("shard"),
        P("shard"),
        P("shard", None),
        P("shard", None, "rep"),
        P("shard", "rep", None),
    )
    return jax.shard_map(body, mesh=mesh, in_specs=in_specs, out_specs=out_specs, check_vma=False)
```

```python
import functools
import math
import jax
import jax.numpy as jnp
from jax import lax
from jax.experimental import pallas as pl
from jax.experimental.pallas import tpu as pltpu
from jax.sharding import PartitionSpec as P

HEADS = 12
BUCKETS = 32
MAX_DISTANCE = 128
LONGEST = 512
QB = 256
BIG = 1e9
LANES = 128
FF_TILE = 512
ROW_BLOCK = 384
TILE = 256
CHUNKS = 2
GELU_A = math.sqrt(2 / math.pi)
GELU_B = 0.044715
eps_norm = 1e-06


def bucket_table(distance):
    half_count = BUCKETS // 2
    clipped = jnp.maximum(distance, 0)
    counted = jnp.zeros(distance.shape, jnp.int32)
    for section_number in range(1, half_count):
        threshold = math.ceil(
            half_count * (MAX_DISTANCE / half_count) ** (section_number / half_count)
        )
        counted = counted + (clipped >= threshold).astype(jnp.int32)
    return jnp.where(clipped < half_count, clipped, half_count + counted)


def window_distance():
    span = LONGEST + 2 * QB
    place = jnp.arange(span, dtype=jnp.int32)
    place = jnp.where(place >= LONGEST + QB, place - span, place)
    return LONGEST - place


def bias_rows(table):
    distance = window_distance()
    onehot = bucket_table(distance)[None, :] == jnp.arange(BUCKETS, dtype=jnp.int32)[:, None]
    rows = jnp.sum(
        jnp.where(onehot[None], table.astype(jnp.float32).T[:, :, None], 0.0), axis=1
    )
    return jnp.where(distance[None, :] >= 0, rows, -BIG)


def segment_lanes(segment, width):
    lane = jnp.arange(width, dtype=jnp.int32)[None, :] % (width // 2)
    same = segment[:, None] == lane
    first = lane < 4
    query_lanes = jnp.where(first & same, 1.0, 0.0)
    key_lanes = jnp.where(first, jnp.where(same, 0.0, -BIG), jnp.where(lane < 7, 1.0, 0.0))
    return query_lanes.astype(jnp.bfloat16), key_lanes.astype(jnp.bfloat16)


def toeplitz(row):
    span = row.shape[-1]
    full = jnp.broadcast_to(row, (QB, span))
    return pltpu.roll(full, 0, 1, stride=1, stride_axis=0)[:, : LONGEST + QB]


def nt(a, b):
    return lax.dot_general(a, b, (((1,), (1,)), ((), ())), preferred_element_type=jnp.float32)


def nn(a, b):
    return jnp.dot(a, b, preferred_element_type=jnp.float32)


def tn(a, b):
    return lax.dot_general(a, b, (((0,), (0,)), ((), ())), preferred_element_type=jnp.float32)


def forward_kernel(q_ref, k_ref, v_ref, ql_ref, kl_ref, row_ref, out_ref, lse_ref):
    pair = pl.program_id(0)
    length, width = q_ref.shape
    half = width // 2
    window = LONGEST + QB
    lane = lax.broadcasted_iota(jnp.int32, (QB, width), 1)
    lane_k = lax.broadcasted_iota(jnp.int32, (length, width), 1)

    @pl.when(pair == 0)
    def _():
        lse_ref[...] = jnp.zeros_like(lse_ref)

    biases = [toeplitz(row_ref[0, h : h + 1, :]) for h in range(2)]
    keys = [
        jnp.where((lane_k < half) == (h == 0), k_ref[...], kl_ref[...]) for h in range(2)
    ]
    units = [(start, h) for start in range(0, length, QB) for h in range(2)]

    def scores(start, h):
        low = max(0, start - LONGEST)
        q = (q_ref[start : start + QB, :].astype(jnp.float32) * (half**-0.5)).astype(jnp.bfloat16)
        q_own = jnp.where((lane < half) == (h == 0), q, ql_ref[start : start + QB, :])
        wide = start + QB - low
        return nt(q_own, keys[h][low : start + QB, :]) + biases[h][:, window - wide :]

    ahead = scores(*units[0])
    kept = None
    for place, (start, h) in enumerate(units):
        s = ahead
        if place + 1 < len(units):
            ahead = scores(*units[place + 1])
        stop = start + QB
        low = max(0, start - LONGEST)
        peak = jnp.max(s, axis=1, keepdims=True)
        p = jnp.exp(s - peak)
        total = jnp.sum(p, axis=1, keepdims=True)
        o = nn(p.astype(jnp.bfloat16), v_ref[low:stop, :]) * (1.0 / total)
        lse_ref[start:stop, :] += jnp.where(lane == 2 * pair + h, peak + jnp.log(total), 0.0)
        if h == 0:
            kept = o
        else:
            out_ref[start:stop, :] = jnp.where(lane < half, kept, o).astype(jnp.bfloat16)


def attention_forward(qk, v, query_lanes, key_lanes, rows):
    length, model = v.shape
    pairs = HEADS // 2
    width = model // pairs
    span = rows.shape[-1]
    return pl.pallas_call(
        forward_kernel,
        grid=(pairs,),
        in_specs=[
            pl.BlockSpec((length, width), lambda p: (0, p)),
            pl.BlockSpec((length, width), lambda p: (0, p + pairs)),
            pl.BlockSpec((length, width), lambda p: (0, p)),
            pl.BlockSpec((length, width), lambda p: (0, 0)),
            pl.BlockSpec((length, width), lambda p: (0, 0)),
            pl.BlockSpec((1, 2, span), lambda p: (p, 0, 0)),
        ],
        out_specs=[
            pl.BlockSpec((length, width), lambda p: (0, p)),
            pl.BlockSpec((length, width), lambda p: (0, 0)),
        ],
        out_shape=[
            jax.ShapeDtypeStruct((length, model), jnp.bfloat16),
            jax.ShapeDtypeStruct((length, width), jnp.float32),
        ],
        compiler_params=pltpu.CompilerParams(
            dimension_semantics=("arbitrary",), vmem_limit_bytes=40 * 1024 * 1024
        ),
        cost_estimate=pl.CostEstimate(
            flops=1024, bytes_accessed=1024, transcendentals=0
        ),
        name="attention_forward",
    )(qk, qk, v, query_lanes, key_lanes, rows.reshape(pairs, 2, span))


def three_parts(column):
    first = column.astype(jnp.bfloat16).astype(jnp.float32)
    rest = column - first
    second = rest.astype(jnp.bfloat16).astype(jnp.float32)
    return first, second, rest - second


def with_column(lane, half, base, column):
    a, b, c = three_parts(column)
    spare = lane % half
    packed = jnp.where(spare == 4, a, jnp.where(spare == 5, b, jnp.where(spare == 6, c, base)))
    return packed.astype(jnp.bfloat16)


def backward_kernel(
    q_ref, k_ref, v_ref, o_ref, g_ref, ql_ref, kl_ref, row_ref, lse_ref,
    grad_ref, table_ref, dk_acc, dv_acc, diag_acc,
):
    pair = pl.program_id(0)
    length, width = q_ref.shape
    half = width // 2
    window = LONGEST + QB
    lane = lax.broadcasted_iota(jnp.int32, (QB, width), 1)
    lane_k = lax.broadcasted_iota(jnp.int32, (length, width), 1)
    dk_acc[...] = jnp.zeros_like(dk_acc)
    dv_acc[...] = jnp.zeros_like(dv_acc)
    diag_acc[...] = jnp.zeros_like(diag_acc)
    zero = jnp.zeros((), jnp.bfloat16)
    biases = [toeplitz(row_ref[0, h : h + 1, :]).T for h in range(2)]
    owned_k = [(lane_k < half) == (h == 0) for h in range(2)]
    keys = [jnp.where(owned_k[h], k_ref[...], kl_ref[...]) for h in range(2)]
    bare_keys = [jnp.where(owned_k[h], k_ref[...], zero) for h in range(2)]
    values = [jnp.where(owned_k[h], v_ref[...], kl_ref[...]) for h in range(2)]
    units = [(start, h) for start in range(0, length, QB) for h in range(2)]

    def products(start, h):
        low = max(0, start - LONGEST)
        stop = start + QB
        wide = stop - low
        q = (q_ref[start:stop, :].astype(jnp.float32) * (half**-0.5)).astype(jnp.bfloat16)
        g = g_ref[start:stop, :]
        dot_all = g.astype(jnp.float32) * o_ref[start:stop, :].astype(jnp.float32)
        lse_all = lse_ref[start:stop, :]
        q_lanes = ql_ref[start:stop, :].astype(jnp.float32)
        mine = (lane < half) == (h == 0)
        lse = jnp.sum(jnp.where(lane == 2 * pair + h, lse_all, 0.0), axis=1, keepdims=True)
        dot = jnp.sum(jnp.where(mine, dot_all, 0.0), axis=1, keepdims=True)
        q_own = jnp.where(mine, q, with_column(lane, half, q_lanes, -lse))
        g_own = jnp.where(mine, g, with_column(lane, half, jnp.zeros_like(q_lanes), -dot))
        s = nt(keys[h][low:stop, :], q_own) + biases[h][window - wide :, :]
        dp = nt(values[h][low:stop, :], g_own)
        return s, dp, jnp.where(mine, q, zero), jnp.where(mine, g, zero)

    ahead = products(*units[0])
    turned = None
    for place, (start, h) in enumerate(units):
        low = max(0, start - LONGEST)
        stop = start + QB
        wide = stop - low
        s, dp, q_bare, g_bare = ahead
        if place + 1 < len(units):
            ahead = products(*units[place + 1])
        p = jnp.exp(s)
        ds = p * dp
        diag_acc[h, window - wide :, :] += ds
        ds_low = ds.astype(jnp.bfloat16)
        dv_acc[low:stop, :] += nn(p.astype(jnp.bfloat16), g_bare)
        dk_acc[low:stop, :] += nn(ds_low, q_bare)
        part = tn(bare_keys[h][low:stop, :], ds_low)
        if h == 0:
            turned = part
        else:
            grad_ref[0, start:stop, :] = ((turned + part) * (half**-0.5)).T.astype(jnp.bfloat16)
    grad_ref[1] = dk_acc[...].astype(jnp.bfloat16)
    grad_ref[2] = dv_acc[...].astype(jnp.bfloat16)
    span = window + QB
    for h in range(2):
        flat = jnp.concatenate([diag_acc[h].T, jnp.zeros((QB, QB), jnp.float32)], axis=1)
        eight = flat[0:8, :]
        for row in range(8, QB, 8):
            eight = eight + pltpu.roll(flat[row : row + 8, :], span - row, 1)
        total = eight[0:1, :]
        for row in range(1, 8):
            total = total + pltpu.roll(eight[row : row + 1, :], span - row, 1)
        table_ref[0, h : h + 1, :] = total


def attention_backward(qk, v, attended, grad_attended, query_lanes, key_lanes, rows, lse):
    length, model = v.shape
    pairs = HEADS // 2
    width = model // pairs
    span = rows.shape[-1]
    block = pl.BlockSpec((length, width), lambda p: (0, p))
    same = pl.BlockSpec((length, width), lambda p: (0, 0))
    low = jax.ShapeDtypeStruct((3, length, model), jnp.bfloat16)
    return pl.pallas_call(
        backward_kernel,
        grid=(pairs,),
        in_specs=[
            block,
            pl.BlockSpec((length, width), lambda p: (0, p + pairs)),
            pl.BlockSpec((length, width), lambda p: (0, p)),
            block,
            block,
            same,
            same,
            pl.BlockSpec((1, 2, span), lambda p: (p, 0, 0)),
            same,
        ],
        out_specs=[
            pl.BlockSpec((3, length, width), lambda p: (0, 0, p)),
            pl.BlockSpec((1, 2, span), lambda p: (p, 0, 0)),
        ],
        out_shape=[low, jax.ShapeDtypeStruct((pairs, 2, span), jnp.float32)],
        scratch_shapes=[
            pltpu.VMEM((length, width), jnp.float32),
            pltpu.VMEM((length, width), jnp.float32),
            pltpu.VMEM((2, LONGEST + QB, QB), jnp.float32),
        ],
        compiler_params=pltpu.CompilerParams(
            dimension_semantics=("arbitrary",), vmem_limit_bytes=48 * 1024 * 1024
        ),
        cost_estimate=pl.CostEstimate(
            flops=1024, bytes_accessed=1024, transcendentals=0
        ),
        name="attention_backward",
    )(
        qk, qk, v, attended, grad_attended, query_lanes, key_lanes,
        rows.reshape(pairs, 2, span), lse,
    )


def table_gradient(diagonals):
    distance = window_distance()
    onehot = (bucket_table(distance)[:, None] == jnp.arange(BUCKETS, dtype=jnp.int32)[None, :]) & (
        distance >= 0
    )[:, None]
    flat = diagonals.reshape(HEADS, -1)
    return jnp.sum(jnp.where(onehot[:, :, None], flat.T[:, None, :], 0.0), axis=0)


def expert_forward_kernel(
    me_ref, x_ref, g_ref, sum_ref, in_ref, out_ref, router_ref, *refs
):
    y_ref, active_ref, gated_ref, slope_ref, logit_ref, router_grad_ref = refs[-6:]
    step = pl.program_id(0)
    model, hidden = in_ref.shape
    rows = x_ref.shape[0] * x_ref.shape[1]
    x = x_ref[...].reshape(rows, model)
    grad = g_ref[...].reshape(rows, model).astype(jnp.float32)
    id_sum = sum_ref[...].reshape(rows, LANES).astype(jnp.float32)
    me = me_ref[0].astype(jnp.float32)
    lane = lax.broadcasted_iota(jnp.int32, (rows, LANES), 1)
    expert = (lane % (LANES // 2)).astype(jnp.float32)
    own = expert == me
    other = expert == id_sum - me
    first = lane < LANES // 2
    logits = nn(x, router_ref[...])
    own_logit = jnp.sum(jnp.where(first & own, logits, 0.0), axis=1, keepdims=True)
    other_logit = jnp.sum(jnp.where(first & other, logits, 0.0), axis=1, keepdims=True)
    gate = 1.0 / (1.0 + jnp.exp(other_logit - own_logit))
    other_gate = 1.0 / (1.0 + jnp.exp(own_logit - other_logit))
    gated_ref[...] = (gate * grad).astype(jnp.bfloat16)
    result = None
    ahead = nn(x, in_ref[:, :FF_TILE])
    for low in range(0, hidden, FF_TILE):
        high = low + FF_TILE
        v = ahead
        if high < hidden:
            ahead = nn(x, in_ref[:, high : high + FF_TILE])
        square = v * v
        t = jnp.tanh(v * (GELU_A + GELU_A * GELU_B * square))
        h = 0.5 + 0.5 * t
        a = v * h
        slope = h + (a * (1.0 - h)) * (2.0 * GELU_A + 6.0 * GELU_A * GELU_B * square)
        slope_ref[:, low:high] = (gate * slope).astype(jnp.bfloat16)
        a = a.astype(jnp.bfloat16)
        active_ref[:, low:high] = a
        part = nn(a, out_ref[low:high, :])
        result = part if result is None else result + part
    y_ref[...] = (gate * result).astype(jnp.bfloat16).reshape(y_ref.shape)
    gate_grad = jnp.sum(grad * result, axis=1, keepdims=True)
    weight = gate * other_gate * gate_grad
    logit_grad = jnp.where(own, weight, 0.0) - jnp.where(other, weight, 0.0)
    high = logit_grad.astype(jnp.bfloat16)
    rest = (logit_grad - high.astype(jnp.float32)).astype(jnp.bfloat16)
    logit_low = jnp.where(first, high, rest)
    logit_ref[...] = logit_low
    part = tn(x, logit_low)

    @pl.when(step == 0)
    def _():
        router_grad_ref[...] = part

    @pl.when(step > 0)
    def _():
        router_grad_ref[...] += part


def expert_backward_kernel(slot_ref, slope_ref, logit_ref, in_ref, router_ref, *refs):
    pre_ref, back_ref = refs[-2:]
    rows, hidden = slope_ref.shape
    back = nt(logit_ref[...], router_ref[...])
    for low in range(0, hidden, FF_TILE):
        high = low + FF_TILE
        d = slot_ref[:, :, low:high].reshape(rows, FF_TILE).astype(jnp.float32)
        pre = (d * slope_ref[:, low:high].astype(jnp.float32)).astype(jnp.bfloat16)
        pre_ref[:, low:high] = pre
        back = back + nt(pre, in_ref[:, low:high])
    back_ref[...] = back.astype(jnp.bfloat16).reshape(back_ref.shape)


def low_shape(*dims):
    return jax.ShapeDtypeStruct(dims, jnp.bfloat16)


def expert_forward(me, x, grads, sums, chunk, weight_in, weight_out, router_two, kept):
    experts, half, model = x.shape
    hidden = weight_in.shape[1]
    group = max(1, min(experts, ROW_BLOCK // half))
    rows = group * half
    total = experts * half
    fixed = lambda *dims: pl.BlockSpec(dims, lambda i, m: (0, 0), pipeline_mode=pl.Buffered(1))
    flat = lambda width: pl.BlockSpec((rows, width), lambda i, m: (i, 0))
    steps = experts // group
    joint = lambda width: pl.BlockSpec((rows, width), lambda i, m: (i + chunk * steps, 0))
    return pl.pallas_call(
        expert_forward_kernel,
        grid_spec=pltpu.PrefetchScalarGridSpec(
            num_scalar_prefetch=1,
            grid=(experts // group,),
            in_specs=[
                pl.BlockSpec((group, half, model), lambda i, m: (i, 0, 0)),
                pl.BlockSpec((group, half, model), lambda i, m: (i, chunk, 0)),
                pl.BlockSpec((group, half, LANES), lambda i, m: (i, chunk, 0)),
                fixed(model, hidden),
                fixed(hidden, model),
                fixed(model, LANES),
            ]
            + [pl.BlockSpec(memory_space=pl.ANY)] * len(kept),
            out_specs=[
                pl.BlockSpec((group, half, model), lambda i, m: (i, chunk, 0)),
                joint(hidden),
                joint(model),
                flat(hidden),
                flat(LANES),
                pl.BlockSpec((model, LANES), lambda i, m: (0, 0)),
            ],
        ),
        out_shape=[
            low_shape(experts, CHUNKS * half, model),
            low_shape(CHUNKS * total, hidden),
            low_shape(CHUNKS * total, model),
            low_shape(total, hidden),
            low_shape(total, LANES),
            jax.ShapeDtypeStruct((model, LANES), jnp.float32),
        ],
        compiler_params=pltpu.CompilerParams(
            dimension_semantics=("arbitrary",), vmem_limit_bytes=56 * 1024 * 1024
        ),
        cost_estimate=pl.CostEstimate(
            flops=4 * total * model * hidden,
            bytes_accessed=4 * total * hidden + 4 * model * hidden + 8 * total * model,
            transcendentals=total * hidden,
        ),
        input_output_aliases={7 + place: place for place in range(len(kept))},
        name="expert_forward",
    )(me, x, grads, sums, weight_in, weight_out, router_two, *kept)


def expert_backward(
    experts, slot_grad, slope, logit_low, chunk, weight_in, router_two, kept
):
    total, hidden = slope.shape
    model = weight_in.shape[0]
    half = total // experts
    group = max(1, min(experts, ROW_BLOCK // half))
    rows = group * half
    fixed = lambda *dims: pl.BlockSpec(dims, lambda i: (0, 0), pipeline_mode=pl.Buffered(1))
    flat = lambda width: pl.BlockSpec((rows, width), lambda i: (i, 0))
    steps = experts // group
    joint = lambda width: pl.BlockSpec((rows, width), lambda i: (i + chunk * steps, 0))
    return pl.pallas_call(
        expert_backward_kernel,
        grid=(experts // group,),
        in_specs=[
            pl.BlockSpec((group, half, hidden), lambda i: (i, chunk, 0)),
            flat(hidden),
            flat(LANES),
            fixed(model, hidden),
            fixed(model, LANES),
        ]
        + [pl.BlockSpec(memory_space=pl.ANY)] * len(kept),
        out_specs=[joint(hidden), pl.BlockSpec((group, half, model), lambda i: (i, 0, 0))],
        out_shape=[low_shape(CHUNKS * total, hidden), low_shape(experts, half, model)],
        compiler_params=pltpu.CompilerParams(
            dimension_semantics=("arbitrary",), vmem_limit_bytes=56 * 1024 * 1024
        ),
        cost_estimate=pl.CostEstimate(flops=1024, bytes_accessed=1024, transcendentals=0),
        input_output_aliases={5 + place: place for place in range(len(kept))},
        name="expert_backward",
    )(slot_grad, slope, logit_low, weight_in, router_two, *kept)


def swap(values, axis, bit):
    count = lax.axis_size(axis)
    return lax.ppermute(values, axis, [(place, place ^ bit) for place in range(count)])


def bits_of(axis):
    count = lax.axis_size(axis)
    return [1 << place for place in range(count.bit_length() - 1)]


def order_kernel(order_ref, *refs):
    count = len(refs) // 3
    chips = refs[0].shape[0]
    core = order_ref[0]
    for part in range(count):
        near, far, out = refs[2 * part], refs[2 * part + 1], refs[2 * count + part]
        for chip in range(chips):
            source = order_ref[1 + part * chips + chip]
            out[chip, core] = near[source]
            out[chip, 1 - core] = far[source]


def gather_rows(parts, axis, orders):
    held = [part[None] for part in parts]
    offsets = [[0] for _ in parts]
    for stage in range(len(orders[0])):
        for part, order in enumerate(orders):
            bit = order[stage]
            held[part] = jnp.concatenate([held[part], swap(held[part], axis, bit)], axis=0)
            offsets[part] = offsets[part] + [offset ^ bit for offset in offsets[part]]
        if stage == 0:
            early = list(held)
    spread = []
    for part, near in enumerate(held):
        place = [0] * len(offsets[part])
        for index, offset in enumerate(offsets[part]):
            place[offset // 2] = index
        spread.append((near, swap(near, axis, 1), place))
    me = lax.axis_index(axis).astype(jnp.int32)
    chips = spread[0][0].shape[0]
    order = [(me % 2)[None]]
    for _, _, place in spread:
        order.append(
            jnp.asarray(place, jnp.int32)[jnp.arange(chips, dtype=jnp.int32) ^ (me // 2)]
        )
    whole = pl.BlockSpec(memory_space=pltpu.VMEM)
    full = pl.pallas_call(
        order_kernel,
        in_specs=[pl.BlockSpec(memory_space=pltpu.SMEM)] + [whole] * (2 * len(parts)),
        out_specs=[whole] * len(parts),
        out_shape=[
            jax.ShapeDtypeStruct((chips, 2) + part.shape, part.dtype) for part in parts
        ],
        compiler_params=pltpu.CompilerParams(vmem_limit_bytes=24 * 1024 * 1024),
        name="rows_in_order",
    )(jnp.concatenate(order), *(array for near, far, _ in spread for array in (near, far)))
    return [
        array.reshape(2 * chips * part.shape[0], part.shape[1])
        for array, part in zip(full, parts)
    ], early, held


def after(first, *later):
    return lax.optimization_barrier((first, *later))[1:]


def scatter_sum(blocks, axis):
    count, rows, width = blocks.shape
    bits = bits_of(axis)
    me = lax.axis_index(axis)

    def step(values, left, bit):
        at = left.index(bit)
        mine = (me // bit) % 2
        keep = lax.dynamic_index_in_dim(values, mine, at, keepdims=False)
        away = lax.dynamic_index_in_dim(values, 1 - mine, at, keepdims=False)
        came = swap(away, axis, bit)
        total = keep.astype(jnp.float32) + came.astype(jnp.float32)
        return total.astype(jnp.bfloat16), [other for other in left if other != bit]

    left = bits[::-1]
    values = blocks.reshape((2,) * len(bits) + (rows, width))
    values, left = step(values, left, 1)
    stages = [values]
    cut = width // 2
    parts = []
    for half, order in ((values[..., :cut], bits[1:]), (values[..., cut:], bits[:0:-1])):
        remaining = left
        for bit in order:
            half, remaining = step(half, remaining, bit)
            if bit == order[0]:
                stages.append(half)
        parts.append(half)
    return jnp.concatenate(parts, axis=-1), stages


def sum_all(values, axis, beside):
    rows = values.shape[0]
    bits = bits_of(axis)
    mine = lax.axis_index(axis) % 2
    low, high = values[: rows // 2], values[rows // 2 :]
    keep = jnp.where(mine == 0, low, high)
    came = swap(jnp.where(mine == 0, high, low), axis, 1)
    half = (keep.astype(jnp.float32) + came.astype(jnp.float32)).astype(jnp.bfloat16)
    (half,) = after(beside, half)
    for bit in bits[1:]:
        came = swap(half, axis, bit)
        half = (half.astype(jnp.float32) + came.astype(jnp.float32)).astype(jnp.bfloat16)
    came = swap(half, axis, 1)
    return jnp.concatenate(
        [jnp.where(mine == 0, half, came), jnp.where(mine == 0, came, half)], axis=0
    )


def weight_grad_kernel(steps, left_ref, right_ref, *refs):
    out_ref, turned = refs[-2:]
    step = pl.program_id(0)

    @pl.when(step == 0)
    def _():
        turned[...] = left_ref[...].T

    def product():
        out_ref[...] = nn(turned[...], right_ref[0]).astype(jnp.bfloat16)

    if len(refs) == 2:
        product()
    else:
        pl.when(step < steps)(product)

        @pl.when(step >= steps)
        def _():
            out_ref[...] = refs[0][...]


def weight_grad(left, right, extra=None):
    tokens, model = left.shape
    parts, _, width = right.shape
    cuts = width // TILE
    steps = parts * cuts
    last = steps - 1
    in_specs = [
        pl.BlockSpec((tokens, model), lambda i: (0, 0)),
        pl.BlockSpec(
            (1, tokens, TILE), lambda i: (jnp.minimum(i, last) // cuts, 0, jnp.minimum(i, last) % cuts)
        ),
    ]
    operands = [left, right]
    if extra is not None:
        in_specs.append(pl.BlockSpec((model, TILE), lambda i: (0, jnp.maximum(i - last - 1, 0))))
        operands.append(extra)
        steps = steps + extra.shape[1] // TILE
    return pl.pallas_call(
        functools.partial(weight_grad_kernel, last + 1),
        grid=(steps,),
        in_specs=in_specs,
        out_specs=pl.BlockSpec((model, TILE), lambda i: (0, i)),
        out_shape=jax.ShapeDtypeStruct((model, steps * TILE), jnp.bfloat16),
        scratch_shapes=[pltpu.VMEM((model, tokens), jnp.bfloat16)],
        compiler_params=pltpu.CompilerParams(
            dimension_semantics=("arbitrary",), vmem_limit_bytes=32 * 1024 * 1024
        ),
        cost_estimate=pl.CostEstimate(flops=1024, bytes_accessed=1024, transcendentals=0),
        name="weight_grad",
    )(*operands)


def rms_scale(values, gain_vec):
    mean_square = jnp.mean(values * values, axis=-1, keepdims=True)
    return values * lax.rsqrt(mean_square + eps_norm) * gain_vec


def pick_rows(places, source):
    return jnp.dot(places, source, preferred_element_type=jnp.float32).astype(jnp.bfloat16)


def back_rows(places, slots):
    return jnp.einsum("st,sd->td", places, slots, preferred_element_type=jnp.float32)


def body(
    inputs,
    w_query,
    w_key,
    w_value,
    w_output,
    w_router,
    gain_attn,
    gain_expert,
    rel_bias,
    w_in,
    w_out,
    segment_ids,
    expert_ids,
    out_grad,
):
    tokens_here, model_width = inputs.shape
    experts = lax.axis_size("shard")
    me = lax.axis_index("shard").astype(jnp.int32)
    capacity = 3 * tokens_here // experts
    half = capacity // CHUNKS
    rows_here = w_query.shape[0]
    table_here = rel_bias.shape[0]
    table_at = experts + 2

    small = jnp.concatenate(
        [
            w_router,
            gain_attn[:, None],
            gain_expert[:, None],
            jnp.pad(rel_bias, ((0, rows_here - table_here), (0, 0))),
            jnp.zeros((rows_here, LANES - table_at - HEADS), jnp.bfloat16),
        ],
        axis=1,
    )
    bits = bits_of("shard")
    (first_full, second_full), early, held = gather_rows(
        (
            jnp.concatenate([w_query, w_key, small], axis=1),
            jnp.concatenate([w_value, w_output], axis=1),
        ),
        "shard",
        (bits[1:], bits[:0:-1]),
    )
    qk_full = first_full[:, : 2 * model_width]
    small_full = first_full[:, 2 * model_width :]
    value_full = second_full[:, :model_width]
    output_full = second_full[:, model_width:]
    router_full = small_full[:, :experts]
    gain_one = small_full[:, experts].astype(jnp.float32)
    gain_two = small_full[:, experts + 1].astype(jnp.float32)
    table_full = small_full.reshape(experts, rows_here, LANES)[
        :, :table_here, table_at : table_at + HEADS
    ].reshape(BUCKETS, HEADS)
    router_two = jnp.pad(router_full, ((0, 0), (0, LANES // 2 - experts)))
    router_two = jnp.concatenate([router_two, router_two], axis=1)

    flat_ids = expert_ids.reshape(-1)
    onehot_count = (flat_ids[:, None] == jnp.arange(experts, dtype=jnp.int32)[None, :]).astype(
        jnp.int32
    )
    before = jnp.cumsum(onehot_count, axis=0, dtype=jnp.int32) - onehot_count
    slot_ids = jnp.sum(before * onehot_count, axis=1, dtype=jnp.int32)
    flat_rows = (flat_ids * capacity + slot_ids).reshape(tokens_here, 2)
    def places_of(low, count):
        slots = (
            jnp.arange(experts, dtype=jnp.int32)[:, None] * capacity
            + low
            + jnp.arange(count, dtype=jnp.int32)[None, :]
        ).reshape(-1)
        hit = (slots[:, None] == flat_rows[None, :, 0]) | (slots[:, None] == flat_rows[None, :, 1])
        return hit.astype(jnp.bfloat16)

    places = [places_of(chunk * half, half) for chunk in range(CHUNKS)]
    all_places = places_of(0, capacity)

    id_sum = jnp.sum(expert_ids, axis=1).astype(jnp.float32)
    out_grad_later, id_sum = after(early[0], out_grad, id_sum)
    out_grad_later, id_sum = after(early[1], out_grad_later, id_sum)
    slot_sums = jnp.dot(all_places.astype(jnp.float32), id_sum).reshape(experts, capacity)
    slot_sums = lax.all_to_all(slot_sums, "shard", split_axis=0, concat_axis=0, tiled=True)
    slot_sums = jnp.broadcast_to(
        slot_sums[:, :, None], (experts, capacity, LANES)
    ).astype(jnp.bfloat16)
    grad_send = pick_rows(all_places, out_grad_later).reshape(experts, capacity, model_width)
    grad_send, slot_sums, *held = lax.optimization_barrier((grad_send, slot_sums, *held))
    grad_received = lax.all_to_all(grad_send, "shard", split_axis=0, concat_axis=0, tiled=True)

    inputs_f = inputs.astype(jnp.float32)
    normed = rms_scale(inputs_f, gain_one).astype(jnp.bfloat16)
    qk = jnp.dot(normed, qk_full, preferred_element_type=jnp.float32).astype(jnp.bfloat16)
    value = jnp.dot(normed, value_full, preferred_element_type=jnp.float32).astype(jnp.bfloat16)
    query_lanes, key_lanes = segment_lanes(segment_ids[0], model_width // (HEADS // 2))
    rows = bias_rows(table_full)
    attended, lse = attention_forward(qk, value, query_lanes, key_lanes, rows)
    hidden = inputs_f + jnp.dot(attended, output_full, preferred_element_type=jnp.float32)
    normed_two = rms_scale(hidden, gain_two).astype(jnp.bfloat16)

    normed_two, grad_received = lax.optimization_barrier((normed_two, grad_received))
    weight_in = w_in[0]
    weight_out = w_out[0]
    sends = [pick_rows(places[0], normed_two)]
    (grad_rows,) = after(sends[0], grad_received)
    slot_grad = (
        nt(grad_rows.reshape(-1, model_width), weight_out)
        .astype(jnp.bfloat16)
        .reshape(experts, capacity, -1)
    )
    (normed_two_later,) = after(slot_grad, normed_two)
    sends = sends + [pick_rows(places[k], normed_two_later) for k in range(1, CHUNKS)]
    sent = [
        lax.all_to_all(
            send.reshape(experts, half, model_width),
            "shard",
            split_axis=0,
            concat_axis=0,
            tiled=True,
        )
        for send in sends
    ]
    kept, kept_back = (), ()
    returned = []
    router_part = jnp.zeros((model_width, LANES), jnp.float32)
    for k in range(CHUNKS):
        *kept, slope, logit_low, part = expert_forward(
            me[None],
            sent[k],
            grad_received,
            slot_sums,
            k,
            weight_in,
            weight_out,
            router_two,
            kept,
        )
        router_part = router_part + part
        if k == CHUNKS - 1:
            results, active, gated = kept
            (gated,) = after(returned[0], gated)
            grad_out_part = jnp.einsum(
                "rf,rd->fd", active, gated, preferred_element_type=jnp.float32
            ).astype(jnp.bfloat16)
            out_summed = lax.psum_scatter(grad_out_part, "rep", scatter_dimension=0, tiled=True)
            (slope,) = after(grad_out_part, slope)
        *kept_back, back = expert_backward(
            experts, slot_grad, slope, logit_low, k, weight_in, router_two, kept_back
        )
        returned.append(
            lax.all_to_all(back, "shard", split_axis=0, concat_axis=0, tiled=True)
        )
        if k + 1 < CHUNKS:
            (sent[k + 1],) = after(kept_back[0], sent[k + 1])
    kept = kept_back
    returned[0], grad_pre = lax.optimization_barrier((returned[0], kept[0]))
    rows_in = jnp.concatenate([part.reshape(-1, model_width) for part in sent], axis=0)
    grad_in_part = jnp.einsum(
        "rd,rf->df", rows_in, grad_pre, preferred_element_type=jnp.float32
    ).astype(jnp.bfloat16)
    in_summed = lax.psum_scatter(grad_in_part, "rep", scatter_dimension=1, tiled=True)
    *returned, grad_in_part, results = lax.optimization_barrier(
        (*returned, grad_in_part, results)
    )
    results = lax.all_to_all(results, "shard", split_axis=0, concat_axis=0, tiled=True)

    grad_out = out_grad.astype(jnp.float32)
    grad_normed_two = sum(
        back_rows(places[k], returned[k].reshape(-1, model_width)) for k in range(CHUNKS)
    )
    unused_two, norm_two_pull = jax.vjp(rms_scale, hidden, gain_two)
    grad_hidden_norm, grad_gain_two = norm_two_pull(grad_normed_two)
    grad_hidden = grad_out + grad_hidden_norm
    grad_branch = grad_hidden.astype(jnp.bfloat16)
    grad_attended = jnp.einsum(
        "te,de->td", grad_branch, output_full, preferred_element_type=jnp.float32
    ).astype(jnp.bfloat16)

    grad_qkv, diagonals = attention_backward(
        qk, value, attended, grad_attended, query_lanes, key_lanes, rows, lse
    )
    (grad_qkv,) = after(results, grad_qkv)
    grad_qkv, out_summed = lax.optimization_barrier((grad_qkv, out_summed))
    packed = weight_grad(normed, grad_qkv)
    owned, stages = scatter_sum(packed.reshape(experts, rows_here, packed.shape[1]), "shard")
    grad_qkv, diagonals, grad_branch = after(stages[0], grad_qkv, diagonals, grad_branch)
    (results,) = after(stages[1], results)
    grad_table = table_gradient(diagonals)
    grad_normed = jnp.zeros((tokens_here, model_width), jnp.float32)
    for place, weight in enumerate(
        (qk_full[:, :model_width], qk_full[:, model_width:], value_full)
    ):
        grad_normed = grad_normed + jnp.einsum(
            "te,de->td", grad_qkv[place], weight, preferred_element_type=jnp.float32
        )
    unused_one, norm_one_pull = jax.vjp(rms_scale, inputs_f, gain_one)
    grad_inputs_norm, grad_gain_one = norm_one_pull(grad_normed)
    input_grad = (grad_hidden + grad_inputs_norm).astype(jnp.bfloat16)

    grad_router = router_part[:, :experts] + router_part[
        :, LANES // 2 : LANES // 2 + experts
    ]
    table_rows = jnp.pad(
        grad_table.reshape(experts, table_here, HEADS),
        ((0, 0), (0, rows_here - table_here), (0, 0)),
    ).reshape(model_width, HEADS)
    small_grads = jnp.concatenate(
        [
            grad_router,
            grad_gain_one[:, None],
            grad_gain_two[:, None],
            table_rows,
            jnp.zeros((model_width, TILE - table_at - HEADS), jnp.float32),
        ],
        axis=1,
    )
    second_packed = weight_grad(
        attended, grad_branch[None], small_grads.astype(jnp.bfloat16)
    )
    second_owned, _ = scatter_sum(
        second_packed.reshape(experts, rows_here, second_packed.shape[1]), "shard"
    )
    combined = back_rows(all_places, results.reshape(-1, model_width))
    output = (hidden + combined).astype(jnp.bfloat16)
    owned, in_summed = lax.optimization_barrier((owned, in_summed))
    summed = sum_all(jnp.concatenate([owned, second_owned], axis=1), "rep", output)
    summed = summed.astype(jnp.float32)
    small_sum = summed[:, 4 * model_width :]

    return (
        output,
        input_grad,
        summed[:, :model_width],
        summed[:, model_width : 2 * model_width],
        summed[:, 2 * model_width : 3 * model_width],
        summed[:, 3 * model_width : 4 * model_width],
        small_sum[:, :experts],
        small_sum[:, experts],
        small_sum[:, experts + 1],
        small_sum[:table_here, table_at : table_at + HEADS],
        in_summed.astype(jnp.float32)[None],
        out_summed.astype(jnp.float32)[None],
    )


def solution(mesh):
    in_specs = (
        P(("shard", "rep"), None),
        P("shard", None),
        P("shard", None),
        P("shard", None),
        P("shard", None),
        P("shard", None),
        P("shard"),
        P("shard"),
        P("shard", None),
        P("shard", None, None),
        P("shard", None, None),
        P(("shard", "rep"), None),
        P(("shard", "rep"), None),
        P(("shard", "rep"), None),
    )
    out_specs = (
        P(("shard", "rep"), None),
        P(("shard", "rep"), None),
        P("shard", None),
        P("shard", None),
        P("shard", None),
        P("shard", None),
        P("shard", None),
        P("shard"),
        P("shard"),
        P("shard", None),
        P("shard", None, "rep"),
        P("shard", "rep", None),
    )
    return jax.shard_map(body, mesh=mesh, in_specs=in_specs, out_specs=out_specs, check_vma=False)
```

```python
import functools
import math
import jax
import jax.numpy as jnp
from jax import lax
from jax.experimental import pallas as pl
from jax.experimental.pallas import tpu as pltpu
from jax.sharding import PartitionSpec as P

HEADS = 12
BUCKETS = 32
MAX_DISTANCE = 128
LONGEST = 512
QB = 128
BIG = 1e9
LANES = 128
FF_TILE = 512
ROW_BLOCK = 384
TILE = 256
CHUNKS = 2
GELU_A = math.sqrt(2 / math.pi)
GELU_B = 0.044715
eps_norm = 1e-06


def bucket_table(distance):
    half_count = BUCKETS // 2
    clipped = jnp.maximum(distance, 0)
    counted = jnp.zeros(distance.shape, jnp.int32)
    for section_number in range(1, half_count):
        threshold = math.ceil(
            half_count * (MAX_DISTANCE / half_count) ** (section_number / half_count)
        )
        counted = counted + (clipped >= threshold).astype(jnp.int32)
    return jnp.where(clipped < half_count, clipped, half_count + counted)


def window_distance():
    span = LONGEST + 2 * QB
    place = jnp.arange(span, dtype=jnp.int32)
    place = jnp.where(place >= LONGEST + QB, place - span, place)
    return LONGEST - place


def bias_rows(table):
    distance = window_distance()
    onehot = bucket_table(distance)[None, :] == jnp.arange(BUCKETS, dtype=jnp.int32)[:, None]
    rows = jnp.sum(
        jnp.where(onehot[None], table.astype(jnp.float32).T[:, :, None], 0.0), axis=1
    )
    return jnp.where(distance[None, :] >= 0, rows, -BIG)


def segment_lanes(segment, width):
    lane = jnp.arange(width, dtype=jnp.int32)[None, :] % (width // 2)
    same = segment[:, None] == lane
    first = lane < 4
    query_lanes = jnp.where(first & same, 1.0, 0.0)
    key_lanes = jnp.where(first, jnp.where(same, 0.0, -BIG), jnp.where(lane < 7, 1.0, 0.0))
    return query_lanes.astype(jnp.bfloat16), key_lanes.astype(jnp.bfloat16)


def toeplitz(row):
    span = row.shape[-1]
    full = jnp.broadcast_to(row, (QB, span))
    return pltpu.roll(full, 0, 1, stride=1, stride_axis=0)[:, : LONGEST + QB]


def nt(a, b):
    return lax.dot_general(a, b, (((1,), (1,)), ((), ())), preferred_element_type=jnp.float32)


def nn(a, b):
    return jnp.dot(a, b, preferred_element_type=jnp.float32)


def tn(a, b):
    return lax.dot_general(a, b, (((0,), (0,)), ((), ())), preferred_element_type=jnp.float32)


def forward_kernel(q_ref, k_ref, v_ref, ql_ref, kl_ref, row_ref, out_ref, lse_ref):
    pair = pl.program_id(0)
    length, width = q_ref.shape
    half = width // 2
    window = LONGEST + QB
    lane = lax.broadcasted_iota(jnp.int32, (QB, width), 1)
    lane_k = lax.broadcasted_iota(jnp.int32, (length, width), 1)

    @pl.when(pair == 0)
    def _():
        lse_ref[...] = jnp.zeros_like(lse_ref)

    biases = [toeplitz(row_ref[0, h : h + 1, :]) for h in range(2)]
    keys = [
        jnp.where((lane_k < half) == (h == 0), k_ref[...], kl_ref[...]) for h in range(2)
    ]
    units = [(start, h) for start in range(0, length, QB) for h in range(2)]

    def scores(start, h):
        low = max(0, start - LONGEST)
        q = (q_ref[start : start + QB, :].astype(jnp.float32) * (half**-0.5)).astype(jnp.bfloat16)
        q_own = jnp.where((lane < half) == (h == 0), q, ql_ref[start : start + QB, :])
        wide = start + QB - low
        return nt(q_own, keys[h][low : start + QB, :]) + biases[h][:, window - wide :]

    ahead = scores(*units[0])
    kept = None
    for place, (start, h) in enumerate(units):
        s = ahead
        if place + 1 < len(units):
            ahead = scores(*units[place + 1])
        stop = start + QB
        low = max(0, start - LONGEST)
        peak = jnp.max(s, axis=1, keepdims=True)
        p = jnp.exp(s - peak)
        total = jnp.sum(p, axis=1, keepdims=True)
        o = nn(p.astype(jnp.bfloat16), v_ref[low:stop, :]) * (1.0 / total)
        lse_ref[start:stop, :] += jnp.where(lane == 2 * pair + h, peak + jnp.log(total), 0.0)
        if h == 0:
            kept = o
        else:
            out_ref[start:stop, :] = jnp.where(lane < half, kept, o).astype(jnp.bfloat16)


def attention_forward(qk, v, query_lanes, key_lanes, rows):
    length, model = v.shape
    pairs = HEADS // 2
    width = model // pairs
    span = rows.shape[-1]
    return pl.pallas_call(
        forward_kernel,
        grid=(pairs,),
        in_specs=[
            pl.BlockSpec((length, width), lambda p: (0, p)),
            pl.BlockSpec((length, width), lambda p: (0, p + pairs)),
            pl.BlockSpec((length, width), lambda p: (0, p)),
            pl.BlockSpec((length, width), lambda p: (0, 0)),
            pl.BlockSpec((length, width), lambda p: (0, 0)),
            pl.BlockSpec((1, 2, span), lambda p: (p, 0, 0)),
        ],
        out_specs=[
            pl.BlockSpec((length, width), lambda p: (0, p)),
            pl.BlockSpec((length, width), lambda p: (0, 0)),
        ],
        out_shape=[
            jax.ShapeDtypeStruct((length, model), jnp.bfloat16),
            jax.ShapeDtypeStruct((length, width), jnp.float32),
        ],
        compiler_params=pltpu.CompilerParams(
            dimension_semantics=("arbitrary",), vmem_limit_bytes=40 * 1024 * 1024
        ),
        cost_estimate=pl.CostEstimate(
            flops=1024, bytes_accessed=1024, transcendentals=0
        ),
        name="attention_forward",
    )(qk, qk, v, query_lanes, key_lanes, rows.reshape(pairs, 2, span))


def three_parts(column):
    first = column.astype(jnp.bfloat16).astype(jnp.float32)
    rest = column - first
    second = rest.astype(jnp.bfloat16).astype(jnp.float32)
    return first, second, rest - second


def with_column(lane, half, base, column):
    a, b, c = three_parts(column)
    spare = lane % half
    packed = jnp.where(spare == 4, a, jnp.where(spare == 5, b, jnp.where(spare == 6, c, base)))
    return packed.astype(jnp.bfloat16)


def backward_kernel(
    q_ref, k_ref, v_ref, o_ref, g_ref, ql_ref, kl_ref, row_ref, lse_ref,
    grad_ref, table_ref, dk_acc, dv_acc, diag_acc,
):
    pair = pl.program_id(0)
    length, width = q_ref.shape
    half = width // 2
    window = LONGEST + QB
    lane = lax.broadcasted_iota(jnp.int32, (QB, width), 1)
    lane_k = lax.broadcasted_iota(jnp.int32, (length, width), 1)
    dk_acc[...] = jnp.zeros_like(dk_acc)
    dv_acc[...] = jnp.zeros_like(dv_acc)
    diag_acc[...] = jnp.zeros_like(diag_acc)
    zero = jnp.zeros((), jnp.bfloat16)
    biases = [toeplitz(row_ref[0, h : h + 1, :]).T for h in range(2)]
    owned_k = [(lane_k < half) == (h == 0) for h in range(2)]
    keys = [jnp.where(owned_k[h], k_ref[...], kl_ref[...]) for h in range(2)]
    bare_keys = [jnp.where(owned_k[h], k_ref[...], zero) for h in range(2)]
    values = [jnp.where(owned_k[h], v_ref[...], kl_ref[...]) for h in range(2)]
    units = [(start, h) for start in range(0, length, QB) for h in range(2)]

    def products(start, h):
        low = max(0, start - LONGEST)
        stop = start + QB
        wide = stop - low
        q = (q_ref[start:stop, :].astype(jnp.float32) * (half**-0.5)).astype(jnp.bfloat16)
        g = g_ref[start:stop, :]
        dot_all = g.astype(jnp.float32) * o_ref[start:stop, :].astype(jnp.float32)
        lse_all = lse_ref[start:stop, :]
        q_lanes = ql_ref[start:stop, :].astype(jnp.float32)
        mine = (lane < half) == (h == 0)
        lse = jnp.sum(jnp.where(lane == 2 * pair + h, lse_all, 0.0), axis=1, keepdims=True)
        dot = jnp.sum(jnp.where(mine, dot_all, 0.0), axis=1, keepdims=True)
        q_own = jnp.where(mine, q, with_column(lane, half, q_lanes, -lse))
        g_own = jnp.where(mine, g, with_column(lane, half, jnp.zeros_like(q_lanes), -dot))
        s = nt(keys[h][low:stop, :], q_own) + biases[h][window - wide :, :]
        dp = nt(values[h][low:stop, :], g_own)
        return s, dp, jnp.where(mine, q, zero), jnp.where(mine, g, zero)

    ahead = products(*units[0])
    turned = None
    for place, (start, h) in enumerate(units):
        low = max(0, start - LONGEST)
        stop = start + QB
        wide = stop - low
        s, dp, q_bare, g_bare = ahead
        if place + 1 < len(units):
            ahead = products(*units[place + 1])
        p = jnp.exp(s)
        ds = p * dp
        diag_acc[h, window - wide :, :] += ds
        ds_low = ds.astype(jnp.bfloat16)
        dv_acc[low:stop, :] += nn(p.astype(jnp.bfloat16), g_bare)
        dk_acc[low:stop, :] += nn(ds_low, q_bare)
        part = tn(bare_keys[h][low:stop, :], ds_low)
        if h == 0:
            turned = part
        else:
            grad_ref[0, start:stop, :] = ((turned + part) * (half**-0.5)).T.astype(jnp.bfloat16)
    grad_ref[1] = dk_acc[...].astype(jnp.bfloat16)
    grad_ref[2] = dv_acc[...].astype(jnp.bfloat16)
    span = window + QB
    for h in range(2):
        flat = jnp.concatenate([diag_acc[h].T, jnp.zeros((QB, QB), jnp.float32)], axis=1)
        eight = flat[0:8, :]
        for row in range(8, QB, 8):
            eight = eight + pltpu.roll(flat[row : row + 8, :], span - row, 1)
        total = eight[0:1, :]
        for row in range(1, 8):
            total = total + pltpu.roll(eight[row : row + 1, :], span - row, 1)
        table_ref[0, h : h + 1, :] = total


def attention_backward(qk, v, attended, grad_attended, query_lanes, key_lanes, rows, lse):
    length, model = v.shape
    pairs = HEADS // 2
    width = model // pairs
    span = rows.shape[-1]
    block = pl.BlockSpec((length, width), lambda p: (0, p))
    same = pl.BlockSpec((length, width), lambda p: (0, 0))
    low = jax.ShapeDtypeStruct((3, length, model), jnp.bfloat16)
    return pl.pallas_call(
        backward_kernel,
        grid=(pairs,),
        in_specs=[
            block,
            pl.BlockSpec((length, width), lambda p: (0, p + pairs)),
            pl.BlockSpec((length, width), lambda p: (0, p)),
            block,
            block,
            same,
            same,
            pl.BlockSpec((1, 2, span), lambda p: (p, 0, 0)),
            same,
        ],
        out_specs=[
            pl.BlockSpec((3, length, width), lambda p: (0, 0, p)),
            pl.BlockSpec((1, 2, span), lambda p: (p, 0, 0)),
        ],
        out_shape=[low, jax.ShapeDtypeStruct((pairs, 2, span), jnp.float32)],
        scratch_shapes=[
            pltpu.VMEM((length, width), jnp.float32),
            pltpu.VMEM((length, width), jnp.float32),
            pltpu.VMEM((2, LONGEST + QB, QB), jnp.float32),
        ],
        compiler_params=pltpu.CompilerParams(
            dimension_semantics=("arbitrary",), vmem_limit_bytes=48 * 1024 * 1024
        ),
        cost_estimate=pl.CostEstimate(
            flops=1024, bytes_accessed=1024, transcendentals=0
        ),
        name="attention_backward",
    )(
        qk, qk, v, attended, grad_attended, query_lanes, key_lanes,
        rows.reshape(pairs, 2, span), lse,
    )


def table_gradient(diagonals):
    distance = window_distance()
    onehot = (bucket_table(distance)[:, None] == jnp.arange(BUCKETS, dtype=jnp.int32)[None, :]) & (
        distance >= 0
    )[:, None]
    flat = diagonals.reshape(HEADS, -1)
    return jnp.sum(jnp.where(onehot[:, :, None], flat.T[:, None, :], 0.0), axis=0)


def expert_forward_kernel(
    me_ref, x_ref, g_ref, sum_ref, in_ref, out_ref, router_ref, *refs
):
    y_ref, active_ref, gated_ref, slope_ref, logit_ref, router_grad_ref = refs[-6:]
    step = pl.program_id(0)
    model, hidden = in_ref.shape
    rows = x_ref.shape[0] * x_ref.shape[1]
    x = x_ref[...].reshape(rows, model)
    grad = g_ref[...].reshape(rows, model).astype(jnp.float32)
    id_sum = sum_ref[...].reshape(rows, LANES).astype(jnp.float32)
    me = me_ref[0].astype(jnp.float32)
    lane = lax.broadcasted_iota(jnp.int32, (rows, LANES), 1)
    expert = (lane % (LANES // 2)).astype(jnp.float32)
    own = expert == me
    other = expert == id_sum - me
    first = lane < LANES // 2
    logits = nn(x, router_ref[...])
    own_logit = jnp.sum(jnp.where(first & own, logits, 0.0), axis=1, keepdims=True)
    other_logit = jnp.sum(jnp.where(first & other, logits, 0.0), axis=1, keepdims=True)
    gate = 1.0 / (1.0 + jnp.exp(other_logit - own_logit))
    other_gate = 1.0 / (1.0 + jnp.exp(own_logit - other_logit))
    gated_ref[...] = (gate * grad).astype(jnp.bfloat16)
    result = None
    ahead = nn(x, in_ref[:, :FF_TILE])
    for low in range(0, hidden, FF_TILE):
        high = low + FF_TILE
        v = ahead
        if high < hidden:
            ahead = nn(x, in_ref[:, high : high + FF_TILE])
        square = v * v
        t = jnp.tanh(v * (GELU_A + GELU_A * GELU_B * square))
        h = 0.5 + 0.5 * t
        a = v * h
        slope = h + (a * (1.0 - h)) * (2.0 * GELU_A + 6.0 * GELU_A * GELU_B * square)
        slope_ref[:, low:high] = (gate * slope).astype(jnp.bfloat16)
        a = a.astype(jnp.bfloat16)
        active_ref[:, low:high] = a
        part = nn(a, out_ref[low:high, :])
        result = part if result is None else result + part
    y_ref[...] = (gate * result).astype(jnp.bfloat16).reshape(y_ref.shape)
    gate_grad = jnp.sum(grad * result, axis=1, keepdims=True)
    weight = gate * other_gate * gate_grad
    logit_grad = jnp.where(own, weight, 0.0) - jnp.where(other, weight, 0.0)
    high = logit_grad.astype(jnp.bfloat16)
    rest = (logit_grad - high.astype(jnp.float32)).astype(jnp.bfloat16)
    logit_low = jnp.where(first, high, rest)
    logit_ref[...] = logit_low
    part = tn(x, logit_low)

    @pl.when(step == 0)
    def _():
        router_grad_ref[...] = part

    @pl.when(step > 0)
    def _():
        router_grad_ref[...] += part


def expert_backward_kernel(slot_ref, slope_ref, logit_ref, in_ref, router_ref, *refs):
    pre_ref, back_ref = refs[-2:]
    rows, hidden = slope_ref.shape
    back = nt(logit_ref[...], router_ref[...])
    for low in range(0, hidden, FF_TILE):
        high = low + FF_TILE
        d = slot_ref[:, :, low:high].reshape(rows, FF_TILE).astype(jnp.float32)
        pre = (d * slope_ref[:, low:high].astype(jnp.float32)).astype(jnp.bfloat16)
        pre_ref[:, low:high] = pre
        back = back + nt(pre, in_ref[:, low:high])
    back_ref[...] = back.astype(jnp.bfloat16).reshape(back_ref.shape)


def low_shape(*dims):
    return jax.ShapeDtypeStruct(dims, jnp.bfloat16)


def expert_forward(me, x, grads, sums, chunk, weight_in, weight_out, router_two, kept):
    experts, half, model = x.shape
    hidden = weight_in.shape[1]
    group = max(1, min(experts, ROW_BLOCK // half))
    rows = group * half
    total = experts * half
    fixed = lambda *dims: pl.BlockSpec(dims, lambda i, m: (0, 0), pipeline_mode=pl.Buffered(1))
    flat = lambda width: pl.BlockSpec((rows, width), lambda i, m: (i, 0))
    steps = experts // group
    joint = lambda width: pl.BlockSpec((rows, width), lambda i, m: (i + chunk * steps, 0))
    return pl.pallas_call(
        expert_forward_kernel,
        grid_spec=pltpu.PrefetchScalarGridSpec(
            num_scalar_prefetch=1,
            grid=(experts // group,),
            in_specs=[
                pl.BlockSpec((group, half, model), lambda i, m: (i, 0, 0)),
                pl.BlockSpec((group, half, model), lambda i, m: (i, chunk, 0)),
                pl.BlockSpec((group, half, LANES), lambda i, m: (i, chunk, 0)),
                fixed(model, hidden),
                fixed(hidden, model),
                fixed(model, LANES),
            ]
            + [pl.BlockSpec(memory_space=pl.ANY)] * len(kept),
            out_specs=[
                pl.BlockSpec((group, half, model), lambda i, m: (i, chunk, 0)),
                joint(hidden),
                joint(model),
                flat(hidden),
                flat(LANES),
                pl.BlockSpec((model, LANES), lambda i, m: (0, 0)),
            ],
        ),
        out_shape=[
            low_shape(experts, CHUNKS * half, model),
            low_shape(CHUNKS * total, hidden),
            low_shape(CHUNKS * total, model),
            low_shape(total, hidden),
            low_shape(total, LANES),
            jax.ShapeDtypeStruct((model, LANES), jnp.float32),
        ],
        compiler_params=pltpu.CompilerParams(
            dimension_semantics=("arbitrary",), vmem_limit_bytes=56 * 1024 * 1024
        ),
        cost_estimate=pl.CostEstimate(
            flops=4 * total * model * hidden,
            bytes_accessed=4 * total * hidden + 4 * model * hidden + 8 * total * model,
            transcendentals=total * hidden,
        ),
        input_output_aliases={7 + place: place for place in range(len(kept))},
        name="expert_forward",
    )(me, x, grads, sums, weight_in, weight_out, router_two, *kept)


def expert_backward(
    experts, slot_grad, slope, logit_low, chunk, weight_in, router_two, kept
):
    total, hidden = slope.shape
    model = weight_in.shape[0]
    half = total // experts
    group = max(1, min(experts, ROW_BLOCK // half))
    rows = group * half
    fixed = lambda *dims: pl.BlockSpec(dims, lambda i: (0, 0), pipeline_mode=pl.Buffered(1))
    flat = lambda width: pl.BlockSpec((rows, width), lambda i: (i, 0))
    steps = experts // group
    joint = lambda width: pl.BlockSpec((rows, width), lambda i: (i + chunk * steps, 0))
    return pl.pallas_call(
        expert_backward_kernel,
        grid=(experts // group,),
        in_specs=[
            pl.BlockSpec((group, half, hidden), lambda i: (i, chunk, 0)),
            flat(hidden),
            flat(LANES),
            fixed(model, hidden),
            fixed(model, LANES),
        ]
        + [pl.BlockSpec(memory_space=pl.ANY)] * len(kept),
        out_specs=[joint(hidden), pl.BlockSpec((group, half, model), lambda i: (i, 0, 0))],
        out_shape=[low_shape(CHUNKS * total, hidden), low_shape(experts, half, model)],
        compiler_params=pltpu.CompilerParams(
            dimension_semantics=("arbitrary",), vmem_limit_bytes=56 * 1024 * 1024
        ),
        cost_estimate=pl.CostEstimate(flops=1024, bytes_accessed=1024, transcendentals=0),
        input_output_aliases={5 + place: place for place in range(len(kept))},
        name="expert_backward",
    )(slot_grad, slope, logit_low, weight_in, router_two, *kept)


def swap(values, axis, bit):
    count = lax.axis_size(axis)
    return lax.ppermute(values, axis, [(place, place ^ bit) for place in range(count)])


def bits_of(axis):
    count = lax.axis_size(axis)
    return [1 << place for place in range(count.bit_length() - 1)]


def order_kernel(order_ref, *refs):
    count = len(refs) // 3
    chips = refs[0].shape[0]
    core = order_ref[0]
    for part in range(count):
        near, far, out = refs[2 * part], refs[2 * part + 1], refs[2 * count + part]
        for chip in range(chips):
            source = order_ref[1 + part * chips + chip]
            out[chip, core] = near[source]
            out[chip, 1 - core] = far[source]


def gather_rows(parts, axis, orders):
    held = [part[None] for part in parts]
    offsets = [[0] for _ in parts]
    for stage in range(len(orders[0])):
        for part, order in enumerate(orders):
            bit = order[stage]
            held[part] = jnp.concatenate([held[part], swap(held[part], axis, bit)], axis=0)
            offsets[part] = offsets[part] + [offset ^ bit for offset in offsets[part]]
        if stage == 0:
            early = list(held)
    spread = []
    for part, near in enumerate(held):
        place = [0] * len(offsets[part])
        for index, offset in enumerate(offsets[part]):
            place[offset // 2] = index
        spread.append((near, swap(near, axis, 1), place))
    me = lax.axis_index(axis).astype(jnp.int32)
    chips = spread[0][0].shape[0]
    order = [(me % 2)[None]]
    for _, _, place in spread:
        order.append(
            jnp.asarray(place, jnp.int32)[jnp.arange(chips, dtype=jnp.int32) ^ (me // 2)]
        )
    whole = pl.BlockSpec(memory_space=pltpu.VMEM)
    full = pl.pallas_call(
        order_kernel,
        in_specs=[pl.BlockSpec(memory_space=pltpu.SMEM)] + [whole] * (2 * len(parts)),
        out_specs=[whole] * len(parts),
        out_shape=[
            jax.ShapeDtypeStruct((chips, 2) + part.shape, part.dtype) for part in parts
        ],
        compiler_params=pltpu.CompilerParams(vmem_limit_bytes=24 * 1024 * 1024),
        name="rows_in_order",
    )(jnp.concatenate(order), *(array for near, far, _ in spread for array in (near, far)))
    return [
        array.reshape(2 * chips * part.shape[0], part.shape[1])
        for array, part in zip(full, parts)
    ], early, held


def after(first, *later):
    return lax.optimization_barrier((first, *later))[1:]


def scatter_sum(blocks, axis):
    count, rows, width = blocks.shape
    bits = bits_of(axis)
    me = lax.axis_index(axis)

    def step(values, left, bit):
        at = left.index(bit)
        mine = (me // bit) % 2
        keep = lax.dynamic_index_in_dim(values, mine, at, keepdims=False)
        away = lax.dynamic_index_in_dim(values, 1 - mine, at, keepdims=False)
        came = swap(away, axis, bit)
        total = keep.astype(jnp.float32) + came.astype(jnp.float32)
        return total.astype(jnp.bfloat16), [other for other in left if other != bit]

    left = bits[::-1]
    values = blocks.reshape((2,) * len(bits) + (rows, width))
    values, left = step(values, left, 1)
    stages = [values]
    cut = width // 2
    parts = []
    for half, order in ((values[..., :cut], bits[1:]), (values[..., cut:], bits[:0:-1])):
        remaining = left
        for bit in order:
            half, remaining = step(half, remaining, bit)
            if bit == order[0]:
                stages.append(half)
        parts.append(half)
    return jnp.concatenate(parts, axis=-1), stages


def sum_all(values, axis, beside):
    rows = values.shape[0]
    bits = bits_of(axis)
    mine = lax.axis_index(axis) % 2
    low, high = values[: rows // 2], values[rows // 2 :]
    keep = jnp.where(mine == 0, low, high)
    came = swap(jnp.where(mine == 0, high, low), axis, 1)
    half = (keep.astype(jnp.float32) + came.astype(jnp.float32)).astype(jnp.bfloat16)
    for bit in bits[1:]:
        came = swap(half, axis, bit)
        half = (half.astype(jnp.float32) + came.astype(jnp.float32)).astype(jnp.bfloat16)
    (half,) = after(beside, half)
    came = swap(half, axis, 1)
    total = jnp.concatenate(
        [jnp.where(mine == 0, half, came), jnp.where(mine == 0, came, half)], axis=0
    )
    return total


def weight_grad_kernel(steps, left_ref, right_ref, *refs):
    out_ref, turned = refs[-2:]
    step = pl.program_id(0)

    @pl.when(step == 0)
    def _():
        turned[...] = left_ref[...].T

    def product():
        out_ref[...] = nn(turned[...], right_ref[0]).astype(jnp.bfloat16)

    if len(refs) == 2:
        product()
    else:
        pl.when(step < steps)(product)

        @pl.when(step >= steps)
        def _():
            out_ref[...] = refs[0][...]


def weight_grad(left, right, extra=None):
    tokens, model = left.shape
    parts, _, width = right.shape
    cuts = width // TILE
    steps = parts * cuts
    last = steps - 1
    in_specs = [
        pl.BlockSpec((tokens, model), lambda i: (0, 0)),
        pl.BlockSpec(
            (1, tokens, TILE), lambda i: (jnp.minimum(i, last) // cuts, 0, jnp.minimum(i, last) % cuts)
        ),
    ]
    operands = [left, right]
    if extra is not None:
        in_specs.append(pl.BlockSpec((model, TILE), lambda i: (0, jnp.maximum(i - last - 1, 0))))
        operands.append(extra)
        steps = steps + extra.shape[1] // TILE
    return pl.pallas_call(
        functools.partial(weight_grad_kernel, last + 1),
        grid=(steps,),
        in_specs=in_specs,
        out_specs=pl.BlockSpec((model, TILE), lambda i: (0, i)),
        out_shape=jax.ShapeDtypeStruct((model, steps * TILE), jnp.bfloat16),
        scratch_shapes=[pltpu.VMEM((model, tokens), jnp.bfloat16)],
        compiler_params=pltpu.CompilerParams(
            dimension_semantics=("arbitrary",), vmem_limit_bytes=32 * 1024 * 1024
        ),
        cost_estimate=pl.CostEstimate(flops=1024, bytes_accessed=1024, transcendentals=0),
        name="weight_grad",
    )(*operands)


def norm_back_kernel(
    grad_ref, first_ref, second_ref, x_ref, gain_ref, hidden_ref, out_ref, gain_grad_ref
):
    model = x_ref.shape[1]
    grad = nt(grad_ref[0], first_ref[:, :model])
    grad = grad + nt(grad_ref[1], first_ref[:, model : 2 * model])
    grad = grad + nt(grad_ref[2], second_ref[:, :model])
    x = x_ref[...].astype(jnp.float32)
    scale = lax.rsqrt(jnp.mean(x * x, axis=1, keepdims=True) + eps_norm)
    scaled = grad * gain_ref[...]
    inner = jnp.mean(x * scaled, axis=1, keepdims=True)
    back = scale * scaled - x * (scale * scale * scale * inner)
    out_ref[...] = (hidden_ref[...] + back).astype(jnp.bfloat16)
    part = jnp.sum(grad * x * scale, axis=0, keepdims=True)

    @pl.when(pl.program_id(0) == 0)
    def _():
        gain_grad_ref[...] = part

    @pl.when(pl.program_id(0) > 0)
    def _():
        gain_grad_ref[...] += part


def norm_back(grads, first_full, second_full, inputs, gain, grad_hidden):
    _, tokens, model = grads.shape
    rows = min(TILE, tokens)
    block = pl.BlockSpec((rows, model), lambda i: (i, 0))
    fixed = lambda array: pl.BlockSpec(array.shape, lambda i: (0, 0))
    gain = gain[None]
    return pl.pallas_call(
        norm_back_kernel,
        grid=(tokens // rows,),
        in_specs=[
            pl.BlockSpec((3, rows, model), lambda i: (0, i, 0)),
            fixed(first_full),
            fixed(second_full),
            block,
            fixed(gain),
            block,
        ],
        out_specs=[block, pl.BlockSpec((1, model), lambda i: (0, 0))],
        out_shape=[
            jax.ShapeDtypeStruct((tokens, model), jnp.bfloat16),
            jax.ShapeDtypeStruct((1, model), jnp.float32),
        ],
        compiler_params=pltpu.CompilerParams(
            dimension_semantics=("arbitrary",), vmem_limit_bytes=32 * 1024 * 1024
        ),
        cost_estimate=pl.CostEstimate(flops=1024, bytes_accessed=1024, transcendentals=0),
        name="norm_back",
    )(grads, first_full, second_full, inputs, gain, grad_hidden)


def rms_scale(values, gain_vec):
    mean_square = jnp.mean(values * values, axis=-1, keepdims=True)
    return values * lax.rsqrt(mean_square + eps_norm) * gain_vec


def pick_rows(places, source):
    return jnp.dot(places, source, preferred_element_type=jnp.float32).astype(jnp.bfloat16)


def back_rows(places, slots):
    return jnp.einsum("st,sd->td", places, slots, preferred_element_type=jnp.float32)


def body(
    inputs,
    w_query,
    w_key,
    w_value,
    w_output,
    w_router,
    gain_attn,
    gain_expert,
    rel_bias,
    w_in,
    w_out,
    segment_ids,
    expert_ids,
    out_grad,
):
    tokens_here, model_width = inputs.shape
    experts = lax.axis_size("shard")
    me = lax.axis_index("shard").astype(jnp.int32)
    capacity = 3 * tokens_here // experts
    half = capacity // CHUNKS
    rows_here = w_query.shape[0]
    table_here = rel_bias.shape[0]
    table_at = experts + 2

    small = jnp.concatenate(
        [
            w_router,
            gain_attn[:, None],
            gain_expert[:, None],
            jnp.pad(rel_bias, ((0, rows_here - table_here), (0, 0))),
            jnp.zeros((rows_here, LANES - table_at - HEADS), jnp.bfloat16),
        ],
        axis=1,
    )
    bits = bits_of("shard")
    (first_full, second_full), early, held = gather_rows(
        (
            jnp.concatenate([w_query, w_key, small], axis=1),
            jnp.concatenate([w_value, w_output], axis=1),
        ),
        "shard",
        (bits[1:], bits[:0:-1]),
    )
    qk_full = first_full[:, : 2 * model_width]
    small_full = first_full[:, 2 * model_width :]
    value_full = second_full[:, :model_width]
    output_full = second_full[:, model_width:]
    router_full = small_full[:, :experts]
    gain_one = small_full[:, experts].astype(jnp.float32)
    gain_two = small_full[:, experts + 1].astype(jnp.float32)
    table_full = small_full.reshape(experts, rows_here, LANES)[
        :, :table_here, table_at : table_at + HEADS
    ].reshape(BUCKETS, HEADS)
    router_two = jnp.pad(router_full, ((0, 0), (0, LANES // 2 - experts)))
    router_two = jnp.concatenate([router_two, router_two], axis=1)

    flat_ids = expert_ids.reshape(-1)
    onehot_count = (flat_ids[:, None] == jnp.arange(experts, dtype=jnp.int32)[None, :]).astype(
        jnp.int32
    )
    before = jnp.cumsum(onehot_count, axis=0, dtype=jnp.int32) - onehot_count
    slot_ids = jnp.sum(before * onehot_count, axis=1, dtype=jnp.int32)
    flat_rows = (flat_ids * capacity + slot_ids).reshape(tokens_here, 2)
    def places_of(low, count):
        slots = (
            jnp.arange(experts, dtype=jnp.int32)[:, None] * capacity
            + low
            + jnp.arange(count, dtype=jnp.int32)[None, :]
        ).reshape(-1)
        hit = (slots[:, None] == flat_rows[None, :, 0]) | (slots[:, None] == flat_rows[None, :, 1])
        return hit.astype(jnp.bfloat16)

    places = [places_of(chunk * half, half) for chunk in range(CHUNKS)]
    all_places = places_of(0, capacity)

    id_sum = jnp.sum(expert_ids, axis=1).astype(jnp.float32)
    out_grad_later, id_sum = after(early[0], out_grad, id_sum)
    out_grad_later, id_sum = after(early[1], out_grad_later, id_sum)
    slot_sums = jnp.dot(all_places.astype(jnp.float32), id_sum).reshape(experts, capacity)
    slot_sums = lax.all_to_all(slot_sums, "shard", split_axis=0, concat_axis=0, tiled=True)
    slot_sums = jnp.broadcast_to(
        slot_sums[:, :, None], (experts, capacity, LANES)
    ).astype(jnp.bfloat16)
    grad_send = pick_rows(all_places, out_grad_later).reshape(experts, capacity, model_width)
    grad_send, slot_sums, *held = lax.optimization_barrier((grad_send, slot_sums, *held))
    grad_received = lax.all_to_all(grad_send, "shard", split_axis=0, concat_axis=0, tiled=True)

    inputs_f = inputs.astype(jnp.float32)
    normed = rms_scale(inputs_f, gain_one).astype(jnp.bfloat16)
    qk = jnp.dot(normed, qk_full, preferred_element_type=jnp.float32).astype(jnp.bfloat16)
    value = jnp.dot(normed, value_full, preferred_element_type=jnp.float32).astype(jnp.bfloat16)
    query_lanes, key_lanes = segment_lanes(segment_ids[0], model_width // (HEADS // 2))
    rows = bias_rows(table_full)
    attended, lse = attention_forward(qk, value, query_lanes, key_lanes, rows)
    hidden = inputs_f + jnp.dot(attended, output_full, preferred_element_type=jnp.float32)
    normed_two = rms_scale(hidden, gain_two).astype(jnp.bfloat16)

    normed_two, grad_received = lax.optimization_barrier((normed_two, grad_received))
    weight_in = w_in[0]
    weight_out = w_out[0]
    sends = [pick_rows(places[0], normed_two)]
    (grad_rows,) = after(sends[0], grad_received)
    slot_grad = (
        nt(grad_rows.reshape(-1, model_width), weight_out)
        .astype(jnp.bfloat16)
        .reshape(experts, capacity, -1)
    )
    (normed_two_later,) = after(slot_grad, normed_two)
    sends = sends + [pick_rows(places[k], normed_two_later) for k in range(1, CHUNKS)]
    sent = [
        lax.all_to_all(
            send.reshape(experts, half, model_width),
            "shard",
            split_axis=0,
            concat_axis=0,
            tiled=True,
        )
        for send in sends
    ]
    kept, kept_back = (), ()
    returned = []
    router_part = jnp.zeros((model_width, LANES), jnp.float32)
    for k in range(CHUNKS):
        *kept, slope, logit_low, part = expert_forward(
            me[None],
            sent[k],
            grad_received,
            slot_sums,
            k,
            weight_in,
            weight_out,
            router_two,
            kept,
        )
        router_part = router_part + part
        if k == CHUNKS - 1:
            results, active, gated = kept
            (gated,) = after(returned[0], gated)
            grad_out_part = jnp.einsum(
                "rf,rd->fd", active, gated, preferred_element_type=jnp.float32
            ).astype(jnp.bfloat16)
            out_summed = lax.psum_scatter(grad_out_part, "rep", scatter_dimension=0, tiled=True)
            (slope,) = after(grad_out_part, slope)
        *kept_back, back = expert_backward(
            experts, slot_grad, slope, logit_low, k, weight_in, router_two, kept_back
        )
        returned.append(
            lax.all_to_all(back, "shard", split_axis=0, concat_axis=0, tiled=True)
        )
        if k + 1 < CHUNKS:
            (sent[k + 1],) = after(kept_back[0], sent[k + 1])
    kept = kept_back
    returned[0], grad_pre = lax.optimization_barrier((returned[0], kept[0]))
    rows_in = jnp.concatenate([part.reshape(-1, model_width) for part in sent], axis=0)
    grad_in_part = jnp.einsum(
        "rd,rf->df", rows_in, grad_pre, preferred_element_type=jnp.float32
    ).astype(jnp.bfloat16)
    in_summed = lax.psum_scatter(grad_in_part, "rep", scatter_dimension=1, tiled=True)
    last, grad_in_part, results = lax.optimization_barrier((returned[-1], grad_in_part, results))
    returned[-1] = last
    results = lax.all_to_all(results, "shard", split_axis=0, concat_axis=0, tiled=True)

    grad_out = out_grad.astype(jnp.float32)
    grad_normed_two = sum(
        back_rows(places[k], returned[k].reshape(-1, model_width)) for k in range(CHUNKS)
    )
    unused_two, norm_two_pull = jax.vjp(rms_scale, hidden, gain_two)
    grad_hidden_norm, grad_gain_two = norm_two_pull(grad_normed_two)
    grad_hidden = grad_out + grad_hidden_norm
    grad_branch = grad_hidden.astype(jnp.bfloat16)
    grad_attended = jnp.einsum(
        "te,de->td", grad_branch, output_full, preferred_element_type=jnp.float32
    ).astype(jnp.bfloat16)

    grad_qkv, diagonals = attention_backward(
        qk, value, attended, grad_attended, query_lanes, key_lanes, rows, lse
    )
    grad_qkv, out_summed = lax.optimization_barrier((grad_qkv, out_summed))
    packed = weight_grad(normed, grad_qkv)
    (packed,) = after(results, packed)
    owned, stages = scatter_sum(packed.reshape(experts, rows_here, packed.shape[1]), "shard")
    grad_qkv, diagonals, grad_branch = after(stages[0], grad_qkv, diagonals, grad_branch)
    (results,) = after(stages[1], results)
    grad_table = table_gradient(diagonals)
    input_grad, grad_gain_one = norm_back(
        grad_qkv, first_full, second_full, inputs, gain_one, grad_hidden
    )
    grad_gain_one = grad_gain_one[0]

    grad_router = router_part[:, :experts] + router_part[
        :, LANES // 2 : LANES // 2 + experts
    ]
    table_rows = jnp.pad(
        grad_table.reshape(experts, table_here, HEADS),
        ((0, 0), (0, rows_here - table_here), (0, 0)),
    ).reshape(model_width, HEADS)
    small_grads = jnp.concatenate(
        [
            grad_router,
            grad_gain_one[:, None],
            grad_gain_two[:, None],
            table_rows,
            jnp.zeros((model_width, TILE - table_at - HEADS), jnp.float32),
        ],
        axis=1,
    )
    small_grads = small_grads.astype(jnp.bfloat16)
    small_grads, grad_branch = after(stages[1], small_grads, grad_branch)
    small_grads, grad_branch = after(stages[2], small_grads, grad_branch)
    second_packed = weight_grad(attended, grad_branch[None], small_grads)
    second_owned, _ = scatter_sum(
        second_packed.reshape(experts, rows_here, second_packed.shape[1]), "shard"
    )
    combined = back_rows(all_places, results.reshape(-1, model_width))
    output = (hidden + combined).astype(jnp.bfloat16)
    owned, second_owned, in_summed = lax.optimization_barrier((owned, second_owned, in_summed))
    summed = sum_all(jnp.concatenate([owned, second_owned], axis=1), "rep", output)
    summed = summed.astype(jnp.float32)
    small_sum = summed[:, 4 * model_width :]

    return (
        output,
        input_grad,
        summed[:, :model_width],
        summed[:, model_width : 2 * model_width],
        summed[:, 2 * model_width : 3 * model_width],
        summed[:, 3 * model_width : 4 * model_width],
        small_sum[:, :experts],
        small_sum[:, experts],
        small_sum[:, experts + 1],
        small_sum[:table_here, table_at : table_at + HEADS],
        in_summed.astype(jnp.float32)[None],
        out_summed.astype(jnp.float32)[None],
    )


def solution(mesh):
    in_specs = (
        P(("shard", "rep"), None),
        P("shard", None),
        P("shard", None),
        P("shard", None),
        P("shard", None),
        P("shard", None),
        P("shard"),
        P("shard"),
        P("shard", None),
        P("shard", None, None),
        P("shard", None, None),
        P(("shard", "rep"), None),
        P(("shard", "rep"), None),
        P(("shard", "rep"), None),
    )
    out_specs = (
        P(("shard", "rep"), None),
        P(("shard", "rep"), None),
        P("shard", None),
        P("shard", None),
        P("shard", None),
        P("shard", None),
        P("shard", None),
        P("shard"),
        P("shard"),
        P("shard", None),
        P("shard", None, "rep"),
        P("shard", "rep", None),
    )
    return jax.shard_map(body, mesh=mesh, in_specs=in_specs, out_specs=out_specs, check_vma=False)
```

```python
import functools
import math
import jax
import jax.numpy as jnp
from jax import lax
from jax.experimental import pallas as pl
from jax.experimental.pallas import tpu as pltpu
from jax.sharding import PartitionSpec as P

HEADS = 12
BUCKETS = 32
MAX_DISTANCE = 128
LONGEST = 512
QB = 128
BIG = 1e9
LANES = 128
FF_TILE = 512
ROW_BLOCK = 384
TILE = 256
CHUNKS = 2
GELU_A = math.sqrt(2 / math.pi)
GELU_B = 0.044715
eps_norm = 1e-06


def bucket_table(distance):
    half_count = BUCKETS // 2
    clipped = jnp.maximum(distance, 0)
    counted = jnp.zeros(distance.shape, jnp.int32)
    for section_number in range(1, half_count):
        threshold = math.ceil(
            half_count * (MAX_DISTANCE / half_count) ** (section_number / half_count)
        )
        counted = counted + (clipped >= threshold).astype(jnp.int32)
    return jnp.where(clipped < half_count, clipped, half_count + counted)


def window_distance():
    span = LONGEST + 2 * QB
    place = jnp.arange(span, dtype=jnp.int32)
    place = jnp.where(place >= LONGEST + QB, place - span, place)
    return LONGEST - place


def bias_rows(table):
    distance = window_distance()
    onehot = bucket_table(distance)[None, :] == jnp.arange(BUCKETS, dtype=jnp.int32)[:, None]
    rows = jnp.sum(
        jnp.where(onehot[None], table.astype(jnp.float32).T[:, :, None], 0.0), axis=1
    )
    return jnp.where(distance[None, :] >= 0, rows, -BIG)


def segment_lanes(segment, width):
    lane = jnp.arange(width, dtype=jnp.int32)[None, :] % (width // 2)
    same = segment[:, None] == lane
    first = lane < 4
    query_lanes = jnp.where(first & same, 1.0, 0.0)
    key_lanes = jnp.where(first, jnp.where(same, 0.0, -BIG), jnp.where(lane < 7, 1.0, 0.0))
    return query_lanes.astype(jnp.bfloat16), key_lanes.astype(jnp.bfloat16)


def toeplitz(row):
    span = row.shape[-1]
    full = jnp.broadcast_to(row, (QB, span))
    return pltpu.roll(full, 0, 1, stride=1, stride_axis=0)[:, : LONGEST + QB]


def nt(a, b):
    return lax.dot_general(a, b, (((1,), (1,)), ((), ())), preferred_element_type=jnp.float32)


def nn(a, b):
    return jnp.dot(a, b, preferred_element_type=jnp.float32)


def tn(a, b):
    return lax.dot_general(a, b, (((0,), (0,)), ((), ())), preferred_element_type=jnp.float32)


def forward_kernel(q_ref, k_ref, v_ref, ql_ref, kl_ref, row_ref, out_ref, lse_ref):
    pair = pl.program_id(0)
    length, width = q_ref.shape
    half = width // 2
    window = LONGEST + QB
    lane = lax.broadcasted_iota(jnp.int32, (QB, width), 1)
    lane_k = lax.broadcasted_iota(jnp.int32, (length, width), 1)

    @pl.when(pair == 0)
    def _():
        lse_ref[...] = jnp.zeros_like(lse_ref)

    biases = [toeplitz(row_ref[0, h : h + 1, :]) for h in range(2)]
    keys = [
        jnp.where((lane_k < half) == (h == 0), k_ref[...], kl_ref[...]) for h in range(2)
    ]
    units = [(start, h) for start in range(0, length, QB) for h in range(2)]

    def scores(start, h):
        low = max(0, start - LONGEST)
        q = (q_ref[start : start + QB, :].astype(jnp.float32) * (half**-0.5)).astype(jnp.bfloat16)
        q_own = jnp.where((lane < half) == (h == 0), q, ql_ref[start : start + QB, :])
        wide = start + QB - low
        return nt(q_own, keys[h][low : start + QB, :]) + biases[h][:, window - wide :]

    ahead = scores(*units[0])
    kept = None
    for place, (start, h) in enumerate(units):
        s = ahead
        if place + 1 < len(units):
            ahead = scores(*units[place + 1])
        stop = start + QB
        low = max(0, start - LONGEST)
        peak = jnp.max(s, axis=1, keepdims=True)
        p = jnp.exp(s - peak)
        total = jnp.sum(p, axis=1, keepdims=True)
        o = nn(p.astype(jnp.bfloat16), v_ref[low:stop, :]) * (1.0 / total)
        lse_ref[start:stop, :] += jnp.where(lane == 2 * pair + h, peak + jnp.log(total), 0.0)
        if h == 0:
            kept = o
        else:
            out_ref[start:stop, :] = jnp.where(lane < half, kept, o).astype(jnp.bfloat16)


def attention_forward(qk, v, query_lanes, key_lanes, rows):
    length, model = v.shape
    pairs = HEADS // 2
    width = model // pairs
    span = rows.shape[-1]
    return pl.pallas_call(
        forward_kernel,
        grid=(pairs,),
        in_specs=[
            pl.BlockSpec((length, width), lambda p: (0, p)),
            pl.BlockSpec((length, width), lambda p: (0, p + pairs)),
            pl.BlockSpec((length, width), lambda p: (0, p)),
            pl.BlockSpec((length, width), lambda p: (0, 0)),
            pl.BlockSpec((length, width), lambda p: (0, 0)),
            pl.BlockSpec((1, 2, span), lambda p: (p, 0, 0)),
        ],
        out_specs=[
            pl.BlockSpec((length, width), lambda p: (0, p)),
            pl.BlockSpec((length, width), lambda p: (0, 0)),
        ],
        out_shape=[
            jax.ShapeDtypeStruct((length, model), jnp.bfloat16),
            jax.ShapeDtypeStruct((length, width), jnp.float32),
        ],
        compiler_params=pltpu.CompilerParams(
            dimension_semantics=("arbitrary",), vmem_limit_bytes=40 * 1024 * 1024
        ),
        cost_estimate=pl.CostEstimate(
            flops=1024, bytes_accessed=1024, transcendentals=0
        ),
        name="attention_forward",
    )(qk, qk, v, query_lanes, key_lanes, rows.reshape(pairs, 2, span))


def three_parts(column):
    first = column.astype(jnp.bfloat16).astype(jnp.float32)
    rest = column - first
    second = rest.astype(jnp.bfloat16).astype(jnp.float32)
    return first, second, rest - second


def with_column(lane, half, base, column):
    a, b, c = three_parts(column)
    spare = lane % half
    packed = jnp.where(spare == 4, a, jnp.where(spare == 5, b, jnp.where(spare == 6, c, base)))
    return packed.astype(jnp.bfloat16)


def backward_kernel(
    q_ref, k_ref, v_ref, o_ref, g_ref, ql_ref, kl_ref, row_ref, lse_ref,
    grad_ref, table_ref, dk_acc, dv_acc, diag_acc,
):
    pair = pl.program_id(0)
    length, width = q_ref.shape
    half = width // 2
    window = LONGEST + QB
    lane = lax.broadcasted_iota(jnp.int32, (QB, width), 1)
    lane_k = lax.broadcasted_iota(jnp.int32, (length, width), 1)
    dk_acc[...] = jnp.zeros_like(dk_acc)
    dv_acc[...] = jnp.zeros_like(dv_acc)
    diag_acc[...] = jnp.zeros_like(diag_acc)
    zero = jnp.zeros((), jnp.bfloat16)
    biases = [toeplitz(row_ref[0, h : h + 1, :]).T for h in range(2)]
    owned_k = [(lane_k < half) == (h == 0) for h in range(2)]
    keys = [jnp.where(owned_k[h], k_ref[...], kl_ref[...]) for h in range(2)]
    bare_keys = [jnp.where(owned_k[h], k_ref[...], zero) for h in range(2)]
    values = [jnp.where(owned_k[h], v_ref[...], kl_ref[...]) for h in range(2)]
    units = [(start, h) for start in range(0, length, QB) for h in range(2)]

    def products(start, h):
        low = max(0, start - LONGEST)
        stop = start + QB
        wide = stop - low
        q = (q_ref[start:stop, :].astype(jnp.float32) * (half**-0.5)).astype(jnp.bfloat16)
        g = g_ref[start:stop, :]
        dot_all = g.astype(jnp.float32) * o_ref[start:stop, :].astype(jnp.float32)
        lse_all = lse_ref[start:stop, :]
        q_lanes = ql_ref[start:stop, :].astype(jnp.float32)
        mine = (lane < half) == (h == 0)
        lse = jnp.sum(jnp.where(lane == 2 * pair + h, lse_all, 0.0), axis=1, keepdims=True)
        dot = jnp.sum(jnp.where(mine, dot_all, 0.0), axis=1, keepdims=True)
        q_own = jnp.where(mine, q, with_column(lane, half, q_lanes, -lse))
        g_own = jnp.where(mine, g, with_column(lane, half, jnp.zeros_like(q_lanes), -dot))
        s = nt(keys[h][low:stop, :], q_own) + biases[h][window - wide :, :]
        dp = nt(values[h][low:stop, :], g_own)
        return s, dp, jnp.where(mine, q, zero), jnp.where(mine, g, zero)

    ahead = products(*units[0])
    turned = None
    for place, (start, h) in enumerate(units):
        low = max(0, start - LONGEST)
        stop = start + QB
        wide = stop - low
        s, dp, q_bare, g_bare = ahead
        if place + 1 < len(units):
            ahead = products(*units[place + 1])
        p = jnp.exp(s)
        ds = p * dp
        diag_acc[h, window - wide :, :] += ds
        ds_low = ds.astype(jnp.bfloat16)
        dv_acc[low:stop, :] += nn(p.astype(jnp.bfloat16), g_bare)
        dk_acc[low:stop, :] += nn(ds_low, q_bare)
        part = tn(bare_keys[h][low:stop, :], ds_low)
        if h == 0:
            turned = part
        else:
            grad_ref[0, start:stop, :] = ((turned + part) * (half**-0.5)).T.astype(jnp.bfloat16)
    grad_ref[1] = dk_acc[...].astype(jnp.bfloat16)
    grad_ref[2] = dv_acc[...].astype(jnp.bfloat16)
    span = window + QB
    for h in range(2):
        flat = jnp.concatenate([diag_acc[h].T, jnp.zeros((QB, QB), jnp.float32)], axis=1)
        eight = flat[0:8, :]
        for row in range(8, QB, 8):
            eight = eight + pltpu.roll(flat[row : row + 8, :], span - row, 1)
        total = eight[0:1, :]
        for row in range(1, 8):
            total = total + pltpu.roll(eight[row : row + 1, :], span - row, 1)
        table_ref[0, h : h + 1, :] = total


def attention_backward(qk, v, attended, grad_attended, query_lanes, key_lanes, rows, lse):
    length, model = v.shape
    pairs = HEADS // 2
    width = model // pairs
    span = rows.shape[-1]
    block = pl.BlockSpec((length, width), lambda p: (0, p))
    same = pl.BlockSpec((length, width), lambda p: (0, 0))
    low = jax.ShapeDtypeStruct((3, length, model), jnp.bfloat16)
    return pl.pallas_call(
        backward_kernel,
        grid=(pairs,),
        in_specs=[
            block,
            pl.BlockSpec((length, width), lambda p: (0, p + pairs)),
            pl.BlockSpec((length, width), lambda p: (0, p)),
            block,
            block,
            same,
            same,
            pl.BlockSpec((1, 2, span), lambda p: (p, 0, 0)),
            same,
        ],
        out_specs=[
            pl.BlockSpec((3, length, width), lambda p: (0, 0, p)),
            pl.BlockSpec((1, 2, span), lambda p: (p, 0, 0)),
        ],
        out_shape=[low, jax.ShapeDtypeStruct((pairs, 2, span), jnp.float32)],
        scratch_shapes=[
            pltpu.VMEM((length, width), jnp.float32),
            pltpu.VMEM((length, width), jnp.float32),
            pltpu.VMEM((2, LONGEST + QB, QB), jnp.float32),
        ],
        compiler_params=pltpu.CompilerParams(
            dimension_semantics=("arbitrary",), vmem_limit_bytes=48 * 1024 * 1024
        ),
        cost_estimate=pl.CostEstimate(
            flops=1024, bytes_accessed=1024, transcendentals=0
        ),
        name="attention_backward",
    )(
        qk, qk, v, attended, grad_attended, query_lanes, key_lanes,
        rows.reshape(pairs, 2, span), lse,
    )


def table_gradient(diagonals):
    distance = window_distance()
    onehot = (bucket_table(distance)[:, None] == jnp.arange(BUCKETS, dtype=jnp.int32)[None, :]) & (
        distance >= 0
    )[:, None]
    flat = diagonals.reshape(HEADS, -1)
    return jnp.sum(jnp.where(onehot[:, :, None], flat.T[:, None, :], 0.0), axis=0)


def expert_forward_kernel(
    me_ref, x_ref, g_ref, sum_ref, in_ref, out_ref, router_ref, *refs
):
    y_ref, active_ref, gated_ref, slope_ref, logit_ref, router_grad_ref = refs[-6:]
    step = pl.program_id(0)
    model, hidden = in_ref.shape
    rows = x_ref.shape[0] * x_ref.shape[1]
    x = x_ref[...].reshape(rows, model)
    grad = g_ref[...].reshape(rows, model).astype(jnp.float32)
    id_sum = sum_ref[...].reshape(rows, LANES).astype(jnp.float32)
    me = me_ref[0].astype(jnp.float32)
    lane = lax.broadcasted_iota(jnp.int32, (rows, LANES), 1)
    expert = (lane % (LANES // 2)).astype(jnp.float32)
    own = expert == me
    other = expert == id_sum - me
    first = lane < LANES // 2
    logits = nn(x, router_ref[...])
    own_logit = jnp.sum(jnp.where(first & own, logits, 0.0), axis=1, keepdims=True)
    other_logit = jnp.sum(jnp.where(first & other, logits, 0.0), axis=1, keepdims=True)
    gate = 1.0 / (1.0 + jnp.exp(other_logit - own_logit))
    other_gate = 1.0 / (1.0 + jnp.exp(own_logit - other_logit))
    gated_ref[...] = (gate * grad).astype(jnp.bfloat16)
    result = None
    ahead = nn(x, in_ref[:, :FF_TILE])
    for low in range(0, hidden, FF_TILE):
        high = low + FF_TILE
        v = ahead
        if high < hidden:
            ahead = nn(x, in_ref[:, high : high + FF_TILE])
        square = v * v
        t = jnp.tanh(v * (GELU_A + GELU_A * GELU_B * square))
        h = 0.5 + 0.5 * t
        a = v * h
        a = a.astype(jnp.bfloat16)
        h = h.astype(jnp.bfloat16)
        cubic = (2.0 * GELU_A + 6.0 * GELU_A * GELU_B * square).astype(jnp.bfloat16)
        slope = h + (a * (1.0 - h)) * cubic
        slope_ref[:, low:high] = gate.astype(jnp.bfloat16) * slope
        active_ref[:, low:high] = a
        part = nn(a, out_ref[low:high, :])
        result = part if result is None else result + part
    y_ref[...] = (gate * result).astype(jnp.bfloat16).reshape(y_ref.shape)
    gate_grad = jnp.sum(grad * result, axis=1, keepdims=True)
    weight = gate * other_gate * gate_grad
    logit_grad = jnp.where(own, weight, 0.0) - jnp.where(other, weight, 0.0)
    high = logit_grad.astype(jnp.bfloat16)
    rest = (logit_grad - high.astype(jnp.float32)).astype(jnp.bfloat16)
    logit_low = jnp.where(first, high, rest)
    logit_ref[...] = logit_low
    part = tn(x, logit_low)

    @pl.when(step == 0)
    def _():
        router_grad_ref[...] = part

    @pl.when(step > 0)
    def _():
        router_grad_ref[...] += part


def expert_backward_kernel(slot_ref, slope_ref, logit_ref, in_ref, router_ref, *refs):
    pre_ref, back_ref = refs[-2:]
    rows, hidden = slope_ref.shape
    back = nt(logit_ref[...], router_ref[...])
    for low in range(0, hidden, FF_TILE):
        high = low + FF_TILE
        d = slot_ref[:, :, low:high].reshape(rows, FF_TILE).astype(jnp.float32)
        pre = (d * slope_ref[:, low:high].astype(jnp.float32)).astype(jnp.bfloat16)
        pre_ref[:, low:high] = pre
        back = back + nt(pre, in_ref[:, low:high])
    back_ref[...] = back.astype(jnp.bfloat16).reshape(back_ref.shape)


def low_shape(*dims):
    return jax.ShapeDtypeStruct(dims, jnp.bfloat16)


def expert_forward(me, x, grads, sums, chunk, weight_in, weight_out, router_two, kept):
    experts, half, model = x.shape
    hidden = weight_in.shape[1]
    group = max(1, min(experts, ROW_BLOCK // half))
    rows = group * half
    total = experts * half
    fixed = lambda *dims: pl.BlockSpec(dims, lambda i, m: (0, 0), pipeline_mode=pl.Buffered(1))
    flat = lambda width: pl.BlockSpec((rows, width), lambda i, m: (i, 0))
    steps = experts // group
    joint = lambda width: pl.BlockSpec((rows, width), lambda i, m: (i + chunk * steps, 0))
    return pl.pallas_call(
        expert_forward_kernel,
        grid_spec=pltpu.PrefetchScalarGridSpec(
            num_scalar_prefetch=1,
            grid=(experts // group,),
            in_specs=[
                pl.BlockSpec((group, half, model), lambda i, m: (i, 0, 0)),
                pl.BlockSpec((group, half, model), lambda i, m: (i, chunk, 0)),
                pl.BlockSpec((group, half, LANES), lambda i, m: (i, chunk, 0)),
                fixed(model, hidden),
                fixed(hidden, model),
                fixed(model, LANES),
            ]
            + [pl.BlockSpec(memory_space=pl.ANY)] * len(kept),
            out_specs=[
                pl.BlockSpec((group, half, model), lambda i, m: (i, chunk, 0)),
                joint(hidden),
                joint(model),
                flat(hidden),
                flat(LANES),
                pl.BlockSpec((model, LANES), lambda i, m: (0, 0)),
            ],
        ),
        out_shape=[
            low_shape(experts, CHUNKS * half, model),
            low_shape(CHUNKS * total, hidden),
            low_shape(CHUNKS * total, model),
            low_shape(total, hidden),
            low_shape(total, LANES),
            jax.ShapeDtypeStruct((model, LANES), jnp.float32),
        ],
        compiler_params=pltpu.CompilerParams(
            dimension_semantics=("arbitrary",), vmem_limit_bytes=56 * 1024 * 1024
        ),
        cost_estimate=pl.CostEstimate(
            flops=4 * total * model * hidden,
            bytes_accessed=4 * total * hidden + 4 * model * hidden + 8 * total * model,
            transcendentals=total * hidden,
        ),
        input_output_aliases={7 + place: place for place in range(len(kept))},
        name="expert_forward",
    )(me, x, grads, sums, weight_in, weight_out, router_two, *kept)


def expert_backward(
    experts, slot_grad, slope, logit_low, chunk, weight_in, router_two, kept
):
    total, hidden = slope.shape
    model = weight_in.shape[0]
    half = total // experts
    group = max(1, min(experts, ROW_BLOCK // half))
    rows = group * half
    fixed = lambda *dims: pl.BlockSpec(dims, lambda i: (0, 0), pipeline_mode=pl.Buffered(1))
    flat = lambda width: pl.BlockSpec((rows, width), lambda i: (i, 0))
    steps = experts // group
    joint = lambda width: pl.BlockSpec((rows, width), lambda i: (i + chunk * steps, 0))
    return pl.pallas_call(
        expert_backward_kernel,
        grid=(experts // group,),
        in_specs=[
            pl.BlockSpec((group, half, hidden), lambda i: (i, chunk, 0)),
            flat(hidden),
            flat(LANES),
            fixed(model, hidden),
            fixed(model, LANES),
        ]
        + [pl.BlockSpec(memory_space=pl.ANY)] * len(kept),
        out_specs=[joint(hidden), pl.BlockSpec((group, half, model), lambda i: (i, 0, 0))],
        out_shape=[low_shape(CHUNKS * total, hidden), low_shape(experts, half, model)],
        compiler_params=pltpu.CompilerParams(
            dimension_semantics=("arbitrary",), vmem_limit_bytes=56 * 1024 * 1024
        ),
        cost_estimate=pl.CostEstimate(flops=1024, bytes_accessed=1024, transcendentals=0),
        input_output_aliases={5 + place: place for place in range(len(kept))},
        name="expert_backward",
    )(slot_grad, slope, logit_low, weight_in, router_two, *kept)


def swap(values, axis, bit):
    count = lax.axis_size(axis)
    return lax.ppermute(values, axis, [(place, place ^ bit) for place in range(count)])


def bits_of(axis):
    count = lax.axis_size(axis)
    return [1 << place for place in range(count.bit_length() - 1)]


def order_kernel(order_ref, *refs):
    count = len(refs) // 3
    chips = refs[0].shape[0]
    core = order_ref[0]
    for part in range(count):
        near, far, out = refs[2 * part], refs[2 * part + 1], refs[2 * count + part]
        for chip in range(chips):
            source = order_ref[1 + part * chips + chip]
            out[chip, core] = near[source]
            out[chip, 1 - core] = far[source]


def gather_rows(parts, axis, orders):
    held = [part[None] for part in parts]
    offsets = [[0] for _ in parts]
    for stage in range(len(orders[0])):
        for part, order in enumerate(orders):
            bit = order[stage]
            held[part] = jnp.concatenate([held[part], swap(held[part], axis, bit)], axis=0)
            offsets[part] = offsets[part] + [offset ^ bit for offset in offsets[part]]
        if stage == 0:
            early = list(held)
    spread = []
    for part, near in enumerate(held):
        place = [0] * len(offsets[part])
        for index, offset in enumerate(offsets[part]):
            place[offset // 2] = index
        spread.append((near, swap(near, axis, 1), place))
    me = lax.axis_index(axis).astype(jnp.int32)
    chips = spread[0][0].shape[0]
    order = [(me % 2)[None]]
    for _, _, place in spread:
        order.append(
            jnp.asarray(place, jnp.int32)[jnp.arange(chips, dtype=jnp.int32) ^ (me // 2)]
        )
    whole = pl.BlockSpec(memory_space=pltpu.VMEM)
    full = pl.pallas_call(
        order_kernel,
        in_specs=[pl.BlockSpec(memory_space=pltpu.SMEM)] + [whole] * (2 * len(parts)),
        out_specs=[whole] * len(parts),
        out_shape=[
            jax.ShapeDtypeStruct((chips, 2) + part.shape, part.dtype) for part in parts
        ],
        compiler_params=pltpu.CompilerParams(vmem_limit_bytes=24 * 1024 * 1024),
        name="rows_in_order",
    )(jnp.concatenate(order), *(array for near, far, _ in spread for array in (near, far)))
    return [
        array.reshape(2 * chips * part.shape[0], part.shape[1])
        for array, part in zip(full, parts)
    ], early, held


def after(first, *later):
    return lax.optimization_barrier((first, *later))[1:]


def scatter_sum(blocks, axis):
    count, rows, width = blocks.shape
    bits = bits_of(axis)
    me = lax.axis_index(axis)

    def step(values, left, bit):
        at = left.index(bit)
        mine = (me // bit) % 2
        keep = lax.dynamic_index_in_dim(values, mine, at, keepdims=False)
        away = lax.dynamic_index_in_dim(values, 1 - mine, at, keepdims=False)
        came = swap(away, axis, bit)
        total = keep.astype(jnp.float32) + came.astype(jnp.float32)
        return total.astype(jnp.bfloat16), [other for other in left if other != bit]

    left = bits[::-1]
    values = blocks.reshape((2,) * len(bits) + (rows, width))
    values, left = step(values, left, 1)
    stages = [values]
    cut = width // 2
    parts = []
    for half, order in ((values[..., :cut], bits[1:]), (values[..., cut:], bits[:0:-1])):
        remaining = left
        for bit in order:
            half, remaining = step(half, remaining, bit)
            if bit == order[0]:
                stages.append(half)
        parts.append(half)
    return jnp.concatenate(parts, axis=-1), stages


def sum_all(values, axis, beside):
    rows = values.shape[0]
    bits = bits_of(axis)
    mine = lax.axis_index(axis) % 2
    low, high = values[: rows // 2], values[rows // 2 :]
    keep = jnp.where(mine == 0, low, high)
    came = swap(jnp.where(mine == 0, high, low), axis, 1)
    half = (keep.astype(jnp.float32) + came.astype(jnp.float32)).astype(jnp.bfloat16)
    for bit in bits[1:]:
        came = swap(half, axis, bit)
        half = (half.astype(jnp.float32) + came.astype(jnp.float32)).astype(jnp.bfloat16)
    (half,) = after(beside, half)
    came = swap(half, axis, 1)
    total = jnp.concatenate(
        [jnp.where(mine == 0, half, came), jnp.where(mine == 0, came, half)], axis=0
    )
    return total


def weight_grad_kernel(steps, left_ref, right_ref, *refs):
    out_ref, turned = refs[-2:]
    step = pl.program_id(0)

    @pl.when(step == 0)
    def _():
        turned[...] = left_ref[...].T

    def product():
        out_ref[...] = nn(turned[...], right_ref[0]).astype(jnp.bfloat16)

    if len(refs) == 2:
        product()
    else:
        pl.when(step < steps)(product)

        @pl.when(step >= steps)
        def _():
            out_ref[...] = refs[0][...]


def weight_grad(left, right, extra=None):
    tokens, model = left.shape
    parts, _, width = right.shape
    cuts = width // TILE
    steps = parts * cuts
    last = steps - 1
    in_specs = [
        pl.BlockSpec((tokens, model), lambda i: (0, 0)),
        pl.BlockSpec(
            (1, tokens, TILE), lambda i: (jnp.minimum(i, last) // cuts, 0, jnp.minimum(i, last) % cuts)
        ),
    ]
    operands = [left, right]
    if extra is not None:
        in_specs.append(pl.BlockSpec((model, TILE), lambda i: (0, jnp.maximum(i - last - 1, 0))))
        operands.append(extra)
        steps = steps + extra.shape[1] // TILE
    return pl.pallas_call(
        functools.partial(weight_grad_kernel, last + 1),
        grid=(steps,),
        in_specs=in_specs,
        out_specs=pl.BlockSpec((model, TILE), lambda i: (0, i)),
        out_shape=jax.ShapeDtypeStruct((model, steps * TILE), jnp.bfloat16),
        scratch_shapes=[pltpu.VMEM((model, tokens), jnp.bfloat16)],
        compiler_params=pltpu.CompilerParams(
            dimension_semantics=("arbitrary",), vmem_limit_bytes=32 * 1024 * 1024
        ),
        cost_estimate=pl.CostEstimate(flops=1024, bytes_accessed=1024, transcendentals=0),
        name="weight_grad",
    )(*operands)


def norm_back_kernel(
    grad_ref, first_ref, second_ref, x_ref, gain_ref, hidden_ref, out_ref, gain_grad_ref
):
    model = x_ref.shape[1]
    grad = nt(grad_ref[0], first_ref[:, :model])
    grad = grad + nt(grad_ref[1], first_ref[:, model : 2 * model])
    grad = grad + nt(grad_ref[2], second_ref[:, :model])
    x = x_ref[...].astype(jnp.float32)
    scale = lax.rsqrt(jnp.mean(x * x, axis=1, keepdims=True) + eps_norm)
    scaled = grad * gain_ref[...]
    inner = jnp.mean(x * scaled, axis=1, keepdims=True)
    back = scale * scaled - x * (scale * scale * scale * inner)
    out_ref[...] = (hidden_ref[...] + back).astype(jnp.bfloat16)
    part = jnp.sum(grad * x * scale, axis=0, keepdims=True)

    @pl.when(pl.program_id(0) == 0)
    def _():
        gain_grad_ref[...] = part

    @pl.when(pl.program_id(0) > 0)
    def _():
        gain_grad_ref[...] += part


def norm_back(grads, first_full, second_full, inputs, gain, grad_hidden):
    _, tokens, model = grads.shape
    rows = min(TILE, tokens)
    block = pl.BlockSpec((rows, model), lambda i: (i, 0))
    fixed = lambda array: pl.BlockSpec(array.shape, lambda i: (0, 0))
    gain = gain[None]
    return pl.pallas_call(
        norm_back_kernel,
        grid=(tokens // rows,),
        in_specs=[
            pl.BlockSpec((3, rows, model), lambda i: (0, i, 0)),
            fixed(first_full),
            fixed(second_full),
            block,
            fixed(gain),
            block,
        ],
        out_specs=[block, pl.BlockSpec((1, model), lambda i: (0, 0))],
        out_shape=[
            jax.ShapeDtypeStruct((tokens, model), jnp.bfloat16),
            jax.ShapeDtypeStruct((1, model), jnp.float32),
        ],
        compiler_params=pltpu.CompilerParams(
            dimension_semantics=("arbitrary",), vmem_limit_bytes=32 * 1024 * 1024
        ),
        cost_estimate=pl.CostEstimate(flops=1024, bytes_accessed=1024, transcendentals=0),
        name="norm_back",
    )(grads, first_full, second_full, inputs, gain, grad_hidden)


def rms_scale(values, gain_vec):
    mean_square = jnp.mean(values * values, axis=-1, keepdims=True)
    return values * lax.rsqrt(mean_square + eps_norm) * gain_vec


def pick_rows(places, source):
    return jnp.dot(places, source, preferred_element_type=jnp.float32).astype(jnp.bfloat16)


def back_rows(places, slots):
    return jnp.einsum("st,sd->td", places, slots, preferred_element_type=jnp.float32)


def body(
    inputs,
    w_query,
    w_key,
    w_value,
    w_output,
    w_router,
    gain_attn,
    gain_expert,
    rel_bias,
    w_in,
    w_out,
    segment_ids,
    expert_ids,
    out_grad,
):
    tokens_here, model_width = inputs.shape
    experts = lax.axis_size("shard")
    me = lax.axis_index("shard").astype(jnp.int32)
    capacity = 3 * tokens_here // experts
    half = capacity // CHUNKS
    rows_here = w_query.shape[0]
    table_here = rel_bias.shape[0]
    table_at = experts + 2

    small = jnp.concatenate(
        [
            w_router,
            gain_attn[:, None],
            gain_expert[:, None],
            jnp.pad(rel_bias, ((0, rows_here - table_here), (0, 0))),
            jnp.zeros((rows_here, LANES - table_at - HEADS), jnp.bfloat16),
        ],
        axis=1,
    )
    bits = bits_of("shard")
    (first_full, second_full), early, held = gather_rows(
        (
            jnp.concatenate([w_query, w_key, small], axis=1),
            jnp.concatenate([w_value, w_output], axis=1),
        ),
        "shard",
        (bits[1:], bits[:0:-1]),
    )
    qk_full = first_full[:, : 2 * model_width]
    small_full = first_full[:, 2 * model_width :]
    value_full = second_full[:, :model_width]
    output_full = second_full[:, model_width:]
    router_full = small_full[:, :experts]
    gain_one = small_full[:, experts].astype(jnp.float32)
    gain_two = small_full[:, experts + 1].astype(jnp.float32)
    table_full = small_full.reshape(experts, rows_here, LANES)[
        :, :table_here, table_at : table_at + HEADS
    ].reshape(BUCKETS, HEADS)
    router_two = jnp.pad(router_full, ((0, 0), (0, LANES // 2 - experts)))
    router_two = jnp.concatenate([router_two, router_two], axis=1)

    flat_ids = expert_ids.reshape(-1)
    onehot_count = (flat_ids[:, None] == jnp.arange(experts, dtype=jnp.int32)[None, :]).astype(
        jnp.int32
    )
    before = jnp.cumsum(onehot_count, axis=0, dtype=jnp.int32) - onehot_count
    slot_ids = jnp.sum(before * onehot_count, axis=1, dtype=jnp.int32)
    flat_rows = (flat_ids * capacity + slot_ids).reshape(tokens_here, 2)
    def places_of(low, count):
        slots = (
            jnp.arange(experts, dtype=jnp.int32)[:, None] * capacity
            + low
            + jnp.arange(count, dtype=jnp.int32)[None, :]
        ).reshape(-1)
        hit = (slots[:, None] == flat_rows[None, :, 0]) | (slots[:, None] == flat_rows[None, :, 1])
        return hit.astype(jnp.bfloat16)

    places = [places_of(chunk * half, half) for chunk in range(CHUNKS)]
    all_places = places_of(0, capacity)

    id_sum = jnp.sum(expert_ids, axis=1).astype(jnp.float32)
    out_grad_later, id_sum = after(early[0], out_grad, id_sum)
    out_grad_later, id_sum = after(early[1], out_grad_later, id_sum)
    slot_sums = jnp.dot(all_places.astype(jnp.float32), id_sum).reshape(experts, capacity)
    slot_sums = lax.all_to_all(slot_sums, "shard", split_axis=0, concat_axis=0, tiled=True)
    slot_sums = jnp.broadcast_to(
        slot_sums[:, :, None], (experts, capacity, LANES)
    ).astype(jnp.bfloat16)
    grad_send = pick_rows(all_places, out_grad_later).reshape(experts, capacity, model_width)
    grad_send, slot_sums, *held = lax.optimization_barrier((grad_send, slot_sums, *held))
    grad_received = lax.all_to_all(grad_send, "shard", split_axis=0, concat_axis=0, tiled=True)

    inputs_f = inputs.astype(jnp.float32)
    normed = rms_scale(inputs_f, gain_one).astype(jnp.bfloat16)
    qk = jnp.dot(normed, qk_full, preferred_element_type=jnp.float32).astype(jnp.bfloat16)
    value = jnp.dot(normed, value_full, preferred_element_type=jnp.float32).astype(jnp.bfloat16)
    query_lanes, key_lanes = segment_lanes(segment_ids[0], model_width // (HEADS // 2))
    rows = bias_rows(table_full)
    attended, lse = attention_forward(qk, value, query_lanes, key_lanes, rows)
    hidden = inputs_f + jnp.dot(attended, output_full, preferred_element_type=jnp.float32)
    normed_two = rms_scale(hidden, gain_two).astype(jnp.bfloat16)

    normed_two, grad_received, router_two = lax.optimization_barrier(
        (normed_two, grad_received, router_two)
    )
    weight_in = w_in[0]
    weight_out = w_out[0]
    sends = [pick_rows(places[0], normed_two)]
    (grad_rows,) = after(sends[0], grad_received)
    slot_grad = (
        nt(grad_rows.reshape(-1, model_width), weight_out)
        .astype(jnp.bfloat16)
        .reshape(experts, capacity, -1)
    )
    (normed_two_later,) = after(slot_grad, normed_two)
    sends = sends + [pick_rows(places[k], normed_two_later) for k in range(1, CHUNKS)]
    sent = [
        lax.all_to_all(
            send.reshape(experts, half, model_width),
            "shard",
            split_axis=0,
            concat_axis=0,
            tiled=True,
        )
        for send in sends
    ]
    kept, kept_back = (), ()
    returned = []
    router_part = jnp.zeros((model_width, LANES), jnp.float32)
    for k in range(CHUNKS):
        *kept, slope, logit_low, part = expert_forward(
            me[None],
            sent[k],
            grad_received,
            slot_sums,
            k,
            weight_in,
            weight_out,
            router_two,
            kept,
        )
        router_part = router_part + part
        if k == CHUNKS - 1:
            results, active, gated = kept
            (gated,) = after(returned[0], gated)
            grad_out_part = jnp.einsum(
                "rf,rd->fd", active, gated, preferred_element_type=jnp.float32
            ).astype(jnp.bfloat16)
            out_summed = lax.psum_scatter(grad_out_part, "rep", scatter_dimension=0, tiled=True)
            (slope,) = after(grad_out_part, slope)
        *kept_back, back = expert_backward(
            experts, slot_grad, slope, logit_low, k, weight_in, router_two, kept_back
        )
        returned.append(
            lax.all_to_all(back, "shard", split_axis=0, concat_axis=0, tiled=True)
        )
        if k + 1 < CHUNKS:
            (sent[k + 1],) = after(kept_back[0], sent[k + 1])
    kept = kept_back
    returned[0], grad_pre = lax.optimization_barrier((returned[0], kept[0]))
    rows_in = jnp.concatenate([part.reshape(-1, model_width) for part in sent], axis=0)
    grad_in_part = jnp.einsum(
        "rd,rf->df", rows_in, grad_pre, preferred_element_type=jnp.float32
    ).astype(jnp.bfloat16)
    in_summed = lax.psum_scatter(grad_in_part, "rep", scatter_dimension=1, tiled=True)
    last, grad_in_part, results = lax.optimization_barrier((returned[-1], grad_in_part, results))
    returned[-1] = last
    results = lax.all_to_all(results, "shard", split_axis=0, concat_axis=0, tiled=True)

    grad_out = out_grad.astype(jnp.float32)
    grad_normed_two = sum(
        back_rows(places[k], returned[k].reshape(-1, model_width)) for k in range(CHUNKS)
    )
    unused_two, norm_two_pull = jax.vjp(rms_scale, hidden, gain_two)
    grad_hidden_norm, grad_gain_two = norm_two_pull(grad_normed_two)
    grad_hidden = grad_out + grad_hidden_norm
    grad_branch = grad_hidden.astype(jnp.bfloat16)
    grad_attended = jnp.einsum(
        "te,de->td", grad_branch, output_full, preferred_element_type=jnp.float32
    ).astype(jnp.bfloat16)

    grad_qkv, diagonals = attention_backward(
        qk, value, attended, grad_attended, query_lanes, key_lanes, rows, lse
    )
    grad_qkv, out_summed = lax.optimization_barrier((grad_qkv, out_summed))
    packed = weight_grad(normed, grad_qkv)
    (packed,) = after(results, packed)
    owned, stages = scatter_sum(packed.reshape(experts, rows_here, packed.shape[1]), "shard")
    grad_qkv, diagonals, grad_branch = after(stages[0], grad_qkv, diagonals, grad_branch)
    (results,) = after(stages[1], results)
    grad_table = table_gradient(diagonals)
    input_grad, grad_gain_one = norm_back(
        grad_qkv, first_full, second_full, inputs, gain_one, grad_hidden
    )
    grad_gain_one = grad_gain_one[0]

    grad_router = router_part[:, :experts] + router_part[
        :, LANES // 2 : LANES // 2 + experts
    ]
    table_rows = jnp.pad(
        grad_table.reshape(experts, table_here, HEADS),
        ((0, 0), (0, rows_here - table_here), (0, 0)),
    ).reshape(model_width, HEADS)
    small_grads = jnp.concatenate(
        [
            grad_router,
            grad_gain_one[:, None],
            grad_gain_two[:, None],
            table_rows,
            jnp.zeros((model_width, TILE - table_at - HEADS), jnp.float32),
        ],
        axis=1,
    )
    small_grads = small_grads.astype(jnp.bfloat16)
    small_grads, grad_branch = after(stages[1], small_grads, grad_branch)
    small_grads, grad_branch = after(stages[2], small_grads, grad_branch)
    second_packed = weight_grad(attended, grad_branch[None], small_grads)
    second_owned, _ = scatter_sum(
        second_packed.reshape(experts, rows_here, second_packed.shape[1]), "shard"
    )
    combined = back_rows(all_places, results.reshape(-1, model_width))
    output = (hidden + combined).astype(jnp.bfloat16)
    owned, second_owned, in_summed = lax.optimization_barrier((owned, second_owned, in_summed))
    summed = sum_all(jnp.concatenate([owned, second_owned], axis=1), "rep", output)
    summed = summed.astype(jnp.float32)
    small_sum = summed[:, 4 * model_width :]

    return (
        output,
        input_grad,
        summed[:, :model_width],
        summed[:, model_width : 2 * model_width],
        summed[:, 2 * model_width : 3 * model_width],
        summed[:, 3 * model_width : 4 * model_width],
        small_sum[:, :experts],
        small_sum[:, experts],
        small_sum[:, experts + 1],
        small_sum[:table_here, table_at : table_at + HEADS],
        in_summed.astype(jnp.float32)[None],
        out_summed.astype(jnp.float32)[None],
    )


def solution(mesh):
    in_specs = (
        P(("shard", "rep"), None),
        P("shard", None),
        P("shard", None),
        P("shard", None),
        P("shard", None),
        P("shard", None),
        P("shard"),
        P("shard"),
        P("shard", None),
        P("shard", None, None),
        P("shard", None, None),
        P(("shard", "rep"), None),
        P(("shard", "rep"), None),
        P(("shard", "rep"), None),
    )
    out_specs = (
        P(("shard", "rep"), None),
        P(("shard", "rep"), None),
        P("shard", None),
        P("shard", None),
        P("shard", None),
        P("shard", None),
        P("shard", None),
        P("shard"),
        P("shard"),
        P("shard", None),
        P("shard", None, "rep"),
        P("shard", "rep", None),
    )
    return jax.shard_map(body, mesh=mesh, in_specs=in_specs, out_specs=out_specs, check_vma=False)
```
